256 devices in a mesh: ctx: 32 (over x, z_lo, core), tp: 8 (over z_hi, y).
Axes of the slice: x: 4, y: 4, z: 8 (z_hi: 2, z_lo: 4; z = z_hi * 4 + z_lo), core: 2. Of those that a mesh axis runs over, the one named last changes fastest.
Arguments:
- tokens: bfloat16 [16384, 4096], P('ctx', 'tp'), may hold values from -6 to 6
- norm_gain: float32 [4096], replicated, may hold values from 0.5 to 1.5
- w_in: bfloat16 [4096, 3, 2048], P(None, None, 'tp'), may hold values from -0.09375 to 0.09375
- w_short: float32 [3, 3, 2048], P(None, None, 'tp'), may hold values from -3 to 3
- residues: float32 [2048, 16], P('tp'), may hold values from -0.15625 to 0.15625
- decays: float32 [2048, 16], P('tp'), may hold values from 6.1035156e-05 to 0.05
- direct: float32 [2048], P('tp'), may hold values from -3 to 3
- w_out: bfloat16 [2048, 4096], P('tp'), may hold values from -0.1875 to 0.1875
Outputs:
- mixed: bfloat16 [16384, 4096], P('ctx', 'tp')
The draws below stay inside these ranges and needn't reach their ends.
All inputs are finite; a program needn't handle non-finite values.
Results may differ from the reference program's by a relative error of at most 0.02.
Values may be sent and summed in bfloat16 or wider, within the bound.
A program may use at most 128 MiB of HBM per device.

```python
import math
import jax
import jax.numpy as jnp
from jax import lax

D = 4096
CH = 2048
ORDER = 16
KSHORT = 3
SEQ = 16384
N_TP = 8


def with_spikes(values, key, source, target, blocks, factor):
    owner, partner = [(jnp.arange(values.shape[dim]) // (values.shape[dim] // blocks)).reshape([-1 if axis == dim else 1 for axis in range(values.ndim)]) for dim in (source, target)]
    chosen = jax.random.permutation(key, blocks)[partner]
    strong = (owner == chosen) | (owner == (partner + blocks // 2) % blocks)
    return jnp.where(strong, factor * values, values)


def level_of(stream_key, extent, pieces, least, top_value):
    factor_of = 1.0
    for position, blocks in pieces:
        draws = jax.random.uniform(jax.random.fold_in(jax.random.fold_in(stream_key, 6), position), (blocks,), jnp.float32, least / len(pieces), top_value / len(pieces))
        factor_of = factor_of * jnp.repeat(jnp.exp(draws), extent[position] // blocks).reshape((-1,) + (1,) * (len(extent) - 1 - position))
    return factor_of


def noise(stream_key, shape, scale, bound, shards=(), kind=jnp.bfloat16):
    gain = level_of(stream_key, shape, shards, -0.22, 0.18) if shards else 1.0
    result = jax.random.normal(stream_key, shape, jnp.float32) * scale * gain
    return jnp.minimum(jnp.maximum(result, -bound), bound).astype(kind)


def bell_draw_with(stream_key, dims, scale, most, shards, heavy, dtype=jnp.bfloat16):
    result = scale * jax.random.normal(stream_key, dims, jnp.float32)
    if shards:
        result = result * level_of(stream_key, dims, shards, -0.22, 0.18)
    return jnp.clip(with_spikes(result, jax.random.fold_in(stream_key, 3), *heavy), -most, most).astype(dtype)


def setup_inputs(seed: int = 0) -> dict:
    splits = jax.random.split(jax.random.key(seed), 9)
    return {
        "tokens": noise(splits[0], (SEQ, D), 1.0, 6.0, ((0, 32), (1, 8))),
        "norm_gain": jnp.clip(1.0 + 0.1 * jax.random.normal(splits[1], (D,), jnp.float32), 0.5, 1.5),
        "w_in": noise(splits[2], (D, 3, CH), D ** -0.5, 0.09375, ((2, 8),)),
        "w_short": noise(splits[3], (KSHORT, 3, CH), 0.6, 3.0, ((2, 8),), jnp.float32),
        "residues": noise(splits[4], (CH, ORDER), 0.01, 0.15625, ((0, 8),), jnp.float32),
        "decays": jnp.clip(jnp.exp(math.log(0.05) - 6.7083283 * jax.random.uniform(splits[5], (CH, ORDER), jnp.float32) ** level_of(splits[5], (CH, ORDER), ((0, 8),), -0.2, 0.2)), 6.103515625e-05, 0.05),
        "direct": noise(splits[6], (CH,), 1.0, 3.0, ((0, 8),), jnp.float32),
        "w_out": bell_draw_with(splits[7], (CH, D), CH ** -0.5, 0.1875, ((0, 8),), (0, 1, 8, 2.0)),
    }


def conv_block(operands):
    signal, rate_block, weight_block = operands
    steps = jnp.arange(SEQ).astype(jnp.float32)[:, None]
    filt = jnp.zeros(signal.shape, jnp.float32)
    for order_index in range(ORDER):
        filt = filt + weight_block[:, order_index][None, :] * jnp.exp(-rate_block[:, order_index][None, :] * steps)
    spec_signal = jnp.fft.rfft(signal, n=2 * SEQ, axis=0)
    spec_filt = jnp.fft.rfft(filt, n=2 * SEQ, axis=0)
    return jnp.fft.irfft(spec_signal * spec_filt, n=2 * SEQ, axis=0)[:SEQ]

def reference(tokens, norm_gain, w_in, w_short, residues, decays, direct, w_out):
    values = tokens.astype(jnp.float32)
    meansq = lax.optimization_barrier(jnp.mean(values * values, axis=-1, keepdims=True))
    normed = (values * lax.rsqrt(meansq + 1e-06) * norm_gain[None, :]).astype(jnp.bfloat16)
    proj = jnp.dot(normed, w_in.reshape(D, 3 * CH), preferred_element_type=jnp.float32)
    proj = proj.astype(jnp.bfloat16).reshape(SEQ, 3, CH)
    reach = KSHORT - 1
    padded = jnp.concatenate([jnp.zeros((reach, 3, CH), jnp.bfloat16), proj], axis=0).astype(jnp.float32)
    short = jnp.zeros((SEQ, 3, CH), jnp.float32)
    for tap in range(KSHORT):
        short = short + w_short[tap][None, :, :] * padded[reach - tap:reach - tap + SEQ]
    gate_q = short[:, 0, :]
    mixed_in = short[:, 1, :] * short[:, 2, :]
    block = 128
    blocks = CH // block
    signal = mixed_in.reshape(SEQ, blocks, block).transpose(1, 0, 2)
    rate_blocks = decays.reshape(blocks, block, ORDER)
    weight_blocks = residues.reshape(blocks, block, ORDER)
    convolved = lax.map(conv_block, (signal, rate_blocks, weight_blocks))
    convolved = convolved.transpose(1, 0, 2).reshape(SEQ, CH)
    gated = (gate_q * (convolved + direct[None, :] * mixed_in)).astype(jnp.bfloat16)
    share = CH // N_TP
    total = jnp.zeros((SEQ, D), jnp.float32)
    for group in range(N_TP):
        partial_sum = jnp.dot(gated[:, group * share:(group + 1) * share], w_out[group * share:(group + 1) * share], preferred_element_type=jnp.float32)
        rounded = lax.optimization_barrier(partial_sum.astype(jnp.bfloat16))
        total = total + rounded.astype(jnp.float32)
    return total.astype(jnp.bfloat16)
```

```python
import jax
import jax.numpy as jnp
from jax import lax
from jax.experimental import pallas as pl
from jax.experimental.pallas import tpu as pltpu
from jax.sharding import PartitionSpec as P

MESH = pl.DeviceIdType.MESH
F32 = jnp.float32
BF16 = jnp.bfloat16

X, ZL, CORES = 4, 4, 2
ZH, Y = 2, 4
N_CTX = X * ZL * CORES
N_TP = ZH * Y
ROWS = 512
FEAT = 512
D = 4096
CHL = 256
MODES = 16
PIECES = 4
PROWS = ROWS // PIECES
HALF = PROWS // 2
HALO = 16
EXT = ROWS + HALO
T = 16
NCH = ROWS // T
LANES = 128
HV = CHL // LANES


def remote(src, dst, send, recv, device):
    return pltpu.make_async_remote_copy(
        src_ref=src, dst_ref=dst, send_sem=send, recv_sem=recv, device_id=device, device_id_type=MESH
    )


def kernel(
    tok, gain, w_in, w_short, res, dec, direct, w_out, out,
    xg, halo, wv, xs, ssq, acc, pb, qb, xb, yb, ft, ab, eb, sb, gb, own, gg, wo, oacc,
    st_core, st_z, st_x,
    s1, r1, s2, r2, hs, hr, ws, wr, zs, zr, xsnd, xrcv, cs, cr, es, er, lsem,
):
    ctx = lax.axis_index("ctx")
    tp = lax.axis_index("tp")
    x, zl, core = ctx // (ZL * CORES), (ctx // CORES) % ZL, ctx % CORES
    zh, y = tp // Y, tp % Y

    def at_ctx(xx, zz, cc):
        return ((xx * ZL + zz) * CORES + cc, tp)

    def at_tp(hh, yy):
        return (ctx, hh * Y + yy)

    right, left = at_tp(zh, (y + 1) % Y), at_tp(zh, (y + Y - 1) % Y)
    across = at_tp(1 - zh, y)
    tp_others = [(a, b) for a in range(ZH) for b in range(Y) if a or b]
    tp_dev = [at_tp((zh + a) % ZH, (y + b) % Y) for a, b in tp_others]
    z_dev = [at_ctx(x, (zl + b) % ZL, core) for b in range(1, ZL)]
    x_dev = [at_ctx((x + a) % X, zl, core) for a in range(1, X)]
    other = at_ctx(x, zl, 1 - core)
    after = ((ctx + 1) % N_CTX, tp)
    before = ((ctx + N_CTX - 1) % N_CTX, tp)

    w_load = pltpu.make_async_copy(w_in, wv, lsem.at[0])
    w_load.start()

    barrier = pltpu.get_barrier_semaphore()
    greeted = tp_dev + z_dev + x_dev + [other, after, before]
    for device in greeted:
        pl.semaphore_signal(barrier, inc=1, device_id=device, device_id_type=MESH)
    pl.semaphore_wait(barrier, len(greeted))

    def rows_of(c, half=None):
        start = ROWS - PROWS * (c + 1)
        if half is None:
            return pl.ds(start, PROWS)
        return pl.ds(start + half * HALF, HALF)

    class Gather:
        def __init__(self, mine, buf, send, recv):
            self.mine, self.buf, self.send, self.recv = mine, buf, send, recv

        def held(self, p, s):
            return self.mine if (p, s) == (0, 0) else self.buf.at[p, s]

        def copy(self, kind, p, c):
            if kind == 0:
                src, dst, dev = self.held(p, 0).at[rows_of(c)], self.buf.at[p, 1, rows_of(c)], right
            elif kind == 1:
                src, dst, dev = self.held(p, 0).at[rows_of(c)], self.buf.at[p, 3, rows_of(c)], left
            elif kind == 2:
                src, dst, dev = self.buf.at[p, 1, rows_of(c, 0)], self.buf.at[p, 2, rows_of(c, 0)], right
            elif kind == 3:
                src, dst, dev = self.buf.at[p, 3, rows_of(c, 1)], self.buf.at[p, 2, rows_of(c, 1)], left
            else:
                src, dst, dev = self.mine.at[rows_of(c)], self.buf.at[1, 0, rows_of(c)], across
            return remote(src, dst, self.send.at[kind, p, c], self.recv.at[kind, p, c], dev)

        def cross(self):
            for c in range(PIECES):
                self.copy(4, 0, c).start()

        def spread(self, p, c):
            if p == 1:
                self.copy(4, 0, c).wait_recv()
            self.copy(0, p, c).start()
            self.copy(1, p, c).start()

        def forward(self, p, c):
            self.copy(0, p, c).wait_recv()
            self.copy(2, p, c).start()
            self.copy(1, p, c).wait_recv()
            self.copy(3, p, c).start()

        def arrive(self, p, c):
            self.copy(2, p, c).wait_recv()
            self.copy(3, p, c).wait_recv()

        def sent(self):
            for c in range(PIECES):
                self.copy(4, 0, c).wait_send()
                for p in range(2):
                    for kind in range(4):
                        self.copy(kind, p, c).wait_send()

    def owner(p, s):
        return (zh + p) % ZH * Y + (y + (0, Y - 1, 2, 1)[s]) % Y

    tokens = Gather(tok, xg, s1, r1)

    def halo_copy(p, s):
        return remote(
            tokens.held(p, s).at[pl.ds(ROWS - HALO, HALO)], halo.at[p, s], hs.at[p, s], hr.at[p, s], after
        )

    chip = x * ZL + zl
    lane0 = pl.multiple_of(core * CHL, CHL)

    def wo_first(i):
        a, b = tp_others[i]
        dev = tp_dev[i]
        col = pl.multiple_of(dev[1] * FEAT + core * CHL, CHL)
        rows = pl.ds(pl.multiple_of(chip * HALO, HALO), HALO)
        return remote(
            w_out.at[rows, pl.ds(col, CHL)], wo.at[tp, rows, pl.ds(lane0, CHL)], ws.at[i], wr.at[i], dev
        )

    def wo_mine():
        col = pl.multiple_of(tp * FEAT + core * CHL, CHL)
        rows = pl.ds(pl.multiple_of(chip * HALO, HALO), HALO)
        return pltpu.make_async_copy(w_out.at[rows, pl.ds(col, CHL)], wo.at[tp, rows, pl.ds(lane0, CHL)], lsem.at[1])

    def wo_z(i):
        part = wo.at[:, pl.ds(pl.multiple_of(chip * HALO, HALO), HALO), pl.ds(lane0, CHL)]
        return remote(part, part, zs.at[i], zr.at[i], z_dev[i])

    def wo_x(i):
        part = wo.at[:, pl.ds(pl.multiple_of(x * ZL * HALO, ZL * HALO), ZL * HALO), pl.ds(lane0, CHL)]
        return remote(part, part, xsnd.at[i], xrcv.at[i], x_dev[i])

    def wo_core():
        part = wo.at[:, :, pl.ds(lane0, CHL)]
        return remote(part, part, cs.at[0], cr.at[0], other)

    def project(p, s):
        halo_copy(p, s).wait_recv()
        k = owner(p, s)
        block = tokens.held(p, s)
        scale = jnp.concatenate([gain[pl.ds(4 * k + i, 1), :] for i in range(4)], axis=1)
        head = halo[p, s].astype(F32)
        xs[0:HALO, :] = (head * scale).astype(BF16)
        ssq[0:HALO, :] += sum(jnp.square(head[:, LANES * i:LANES * (i + 1)]) for i in range(4))

        @pl.loop(0, ROWS // 64)
        def _(i):
            at = pl.ds(pl.multiple_of(i * 64, 64), 64)
            to = pl.ds(pl.multiple_of(i * 64 + HALO, HALO), 64)
            values = block[at, :].astype(F32)
            xs[to, :] = (values * scale).astype(BF16)
            ssq[to, :] += sum(jnp.square(values[:, LANES * j:LANES * (j + 1)]) for j in range(4))

        @pl.loop(0, 3)
        def _(g):
            weights = wv[g, pl.ds(pl.multiple_of(k * FEAT, FEAT), FEAT), :]
            acc[g] += jnp.dot(xs[...], weights, preferred_element_type=F32)

    tokens.cross()
    for c in range(PIECES):
        tokens.spread(0, c)
    halo_copy(0, 0).start()
    for i in range(N_TP - 1):
        wo_first(i).start()
    wo_mine().start()

    ssq[...] = jnp.zeros_like(ssq)
    acc[...] = jnp.zeros_like(acc)
    rate = dec[...]
    weight = res[...]
    powers = []
    for lag in range(T):
        row = jnp.sum(weight * jnp.exp(-rate * float(lag)), axis=0, keepdims=True)
        if lag == 0:
            row = row + direct[...]
        for h in range(HV):
            ft[h, lag:lag + 1, :] = row[:, LANES * h:LANES * (h + 1)]
    decay1 = jnp.exp(-rate)
    for h in range(HV):
        ab[h] = decay1[:, LANES * h:LANES * (h + 1)]

    tokens.forward(0, 0)
    halo_copy(0, 1).start()
    halo_copy(0, 3).start()
    w_load.wait()
    project(0, 0)
    tokens.forward(0, 1)
    wo_mine().wait()
    for i in range(N_TP - 1):
        wo_first(i).wait_recv()
    for i in range(ZL - 1):
        wo_z(i).start()
    tokens.spread(1, 0)
    halo_copy(1, 0).start()
    tokens.forward(0, 2)
    tokens.forward(0, 3)
    tokens.arrive(0, 0)
    halo_copy(0, 2).start()
    project(0, 1)
    tokens.spread(1, 1)
    project(0, 3)
    for i in range(ZL - 1):
        wo_z(i).wait_recv()
    for i in range(X - 1):
        wo_x(i).start()
    for c in range(1, PIECES):
        tokens.arrive(0, c)
    tokens.forward(1, 0)
    halo_copy(1, 1).start()
    halo_copy(1, 3).start()
    tokens.spread(1, 2)
    project(0, 2)
    tokens.forward(1, 1)
    tokens.arrive(1, 0)
    halo_copy(1, 2).start()
    tokens.spread(1, 3)
    project(1, 0)
    for i in range(X - 1):
        wo_x(i).wait_recv()
    wo_core().start()
    tokens.forward(1, 2)
    tokens.forward(1, 3)
    project(1, 1)
    project(1, 3)
    for c in range(1, PIECES):
        tokens.arrive(1, c)
    project(1, 2)

    inverse = lax.rsqrt(jnp.sum(ssq[...], axis=1, keepdims=True) * (1.0 / D) + 1e-06)
    row_id = lax.broadcasted_iota(jnp.int32, (EXT, 1), 0)
    inverse = jnp.where((row_id < HALO) & (ctx == 0), 0.0, inverse)
    for g in range(3):
        for h in range(HV):
            pb[g, h] = (acc[g, :, LANES * h:LANES * (h + 1)] * inverse).astype(BF16).astype(F32)

    for h in range(HV):
        lanes = pl.ds(LANES * h, LANES)

        @pl.loop(0, T)
        def _(t):
            streams = []
            for g in range(3):
                total = None
                for j in range(3):
                    plane = pb[g, h, pl.ds(HALO + t - j, NCH, stride=T), :]
                    term = w_short[j, pl.ds(g, 1), lanes] * plane
                    total = term if total is None else total + term
                streams.append(total)
            qb[h, t] = streams[0]
            xb[h, t] = streams[1] * streams[2]

    group = 4
    for h in range(HV):
        for r0 in range(0, MODES, group):
            factors = [jnp.broadcast_to(ab[h, r:r + 1, :], (NCH, LANES)) for r in range(r0, r0 + group)]

            def step(t, states):
                value = xb[h, t]
                return tuple(f * s + value for f, s in zip(factors, states))

            states = lax.fori_loop(0, T, step, tuple(jnp.zeros((NCH, LANES), F32) for _ in factors))
            for i, s in enumerate(states):
                eb[h, (r0 + i) * NCH:(r0 + i + 1) * NCH, :] = s

    block_end = []
    for h in range(HV):
        chunk_decay = jnp.exp(-dec[:, LANES * h:LANES * (h + 1)] * float(T))

        def scan(n, state):
            sb[h, pl.ds(pl.multiple_of(n * MODES, MODES), MODES), :] = state
            return chunk_decay * state + eb[h, pl.ds(n, MODES, stride=NCH), :]

        block_end.append(lax.fori_loop(0, NCH, scan, jnp.zeros((MODES, LANES), F32)))
    mine = jnp.concatenate(block_end, axis=1)

    st_core[0] = mine
    core_copy = remote(st_core.at[0], st_core.at[1], es.at[0], er.at[0], other)
    core_copy.start()
    decay_block = jnp.exp(-dec[...] * float(ROWS))
    decay_chip = jnp.exp(-dec[...] * float(ROWS * CORES))
    decay_line = jnp.exp(-dec[...] * float(ROWS * CORES * ZL))
    core_copy.wait_recv()
    theirs = st_core[1]
    st_z[0] = jnp.where(core == 0, decay_block * mine + theirs, decay_block * theirs + mine)
    z_copies = [
        remote(st_z.at[0], st_z.at[b], es.at[b], er.at[b], z_dev[b - 1]) for b in range(1, ZL)
    ]
    for copy in z_copies:
        copy.start()

    def within(h):
        for t in range(T):
            total = None
            for lag in range(t + 1):
                term = ft[h, lag:lag + 1, :] * xb[h, t - lag]
                total = term if total is None else total + term
            yb[h, t] = total

    within(0)
    for copy in z_copies:
        copy.wait_recv()
    line_end = jnp.zeros((MODES, CHL), F32)
    chip_in = jnp.zeros((MODES, CHL), F32)
    for zz in range(ZL):
        for b in range(ZL):
            here = (zl + ZL - b) % ZL == zz
            piece = st_z[b]
            if b == 0:
                chosen = jnp.where(here, piece, 0.0)
            else:
                chosen = jnp.where(here, piece, chosen)
        line_end = decay_chip * line_end + chosen
        chip_in = jnp.where(zz < zl, decay_chip * chip_in + chosen, chip_in)
    st_x[0] = line_end
    x_copies = [
        remote(st_x.at[0], st_x.at[a], es.at[ZL + a - 1], er.at[ZL + a - 1], x_dev[a - 1]) for a in range(1, X)
    ]
    for copy in x_copies:
        copy.start()
    within(1)
    before_chip = jnp.exp(-dec[...] * (ROWS * CORES * zl).astype(F32))
    for copy in x_copies:
        copy.wait_recv()
    line_in = jnp.zeros((MODES, CHL), F32)
    for xx in range(X):
        for a in range(X):
            here = (x + X - a) % X == xx
            piece = st_x[a]
            if a == 0:
                chosen = jnp.where(here, piece, 0.0)
            else:
                chosen = jnp.where(here, piece, chosen)
        line_in = jnp.where(xx < x, decay_line * line_in + chosen, line_in)
    chip_in = chip_in + before_chip * line_in
    carried = jnp.where(core == 0, chip_in, decay_block * chip_in + theirs)

    for h in range(HV):
        part = slice(LANES * h, LANES * (h + 1))
        chunk_decay = jnp.exp(-dec[:, part] * float(T))
        front = res[:, part] * ab[h]

        def enter(n, state):
            at = pl.ds(pl.multiple_of(n * MODES, MODES), MODES)
            sb[h, at, :] = front * (sb[h, at, :] + state)
            return chunk_decay * state

        lax.fori_loop(0, NCH, enter, carried[:, part])
        for r0 in range(0, MODES, group):
            factors = [jnp.broadcast_to(ab[h, r:r + 1, :], (NCH, LANES)) for r in range(r0, r0 + group)]
            start = tuple(sb[h, pl.ds(r, NCH, stride=MODES), :] for r in range(r0, r0 + group))
            last = r0 + group == MODES

            def step(t, terms):
                total = yb[h, t] + sum(terms[1:], terms[0])
                if last:
                    gb[h, pl.ds(t, NCH, stride=T), :] = qb[h, t] * total
                else:
                    yb[h, t] = total
                return tuple(f * s for f, s in zip(factors, terms))

            lax.fori_loop(0, T, step, start)
    for h in range(HV):
        own[:, LANES * h:LANES * (h + 1)] = gb[h].astype(BF16)

    gates = Gather(own, gg, s2, r2)

    def emit(p, s, first=False, last=False):
        weights = wo[owner(p, s)]
        value = jnp.dot(gates.held(p, s)[...], weights, preferred_element_type=F32)
        if first:
            oacc[...] = value
        elif last:
            out[...] = (oacc[...] + value).astype(BF16)
        else:
            oacc[...] += value

    gates.cross()
    for c in range(PIECES):
        gates.spread(0, c)
    wo_core().wait_recv()
    emit(0, 0, first=True)
    for c in range(PIECES):
        gates.forward(0, c)
        if c >= 2:
            gates.spread(1, c - 2)
    emit(0, 1)
    emit(0, 3)
    for c in range(PIECES):
        gates.arrive(0, c)
    gates.spread(1, 2)
    emit(0, 2)
    gates.forward(1, 0)
    gates.spread(1, 3)
    emit(1, 0)
    for c in range(1, PIECES):
        gates.forward(1, c)
    emit(1, 1)
    emit(1, 3)
    for c in range(PIECES):
        gates.arrive(1, c)
    emit(1, 2, last=True)

    tokens.sent()
    gates.sent()
    for p in range(ZH):
        for s in range(Y):
            halo_copy(p, s).wait_send()
    for i in range(N_TP - 1):
        wo_first(i).wait_send()
    for i in range(ZL - 1):
        wo_z(i).wait_send()
    for i in range(X - 1):
        wo_x(i).wait_send()
    wo_core().wait_send()
    core_copy.wait_send()
    for copy in z_copies + x_copies:
        copy.wait_send()


def local(tokens, norm_gain, w_in, w_short, residues, decays, direct, w_out):
    dma = pltpu.SemaphoreType.DMA
    vmem = pl.BlockSpec(memory_space=pltpu.VMEM)
    hbm = pl.BlockSpec(memory_space=pl.ANY)
    return pl.pallas_call(
        kernel,
        out_shape=jax.ShapeDtypeStruct((ROWS, FEAT), BF16),
        in_specs=[vmem, vmem, hbm, vmem, vmem, vmem, vmem, hbm],
        out_specs=vmem,
        scratch_shapes=[
            pltpu.VMEM((ZH, Y, ROWS, FEAT), BF16),
            pltpu.VMEM((ZH, Y, HALO, FEAT), BF16),
            pltpu.VMEM((3, D, CHL), BF16),
            pltpu.VMEM((EXT, FEAT), BF16),
            pltpu.VMEM((EXT, LANES), F32),
            pltpu.VMEM((3, EXT, CHL), F32),
            pltpu.VMEM((3, HV, EXT, LANES), F32),
            pltpu.VMEM((HV, T, NCH, LANES), F32),
            pltpu.VMEM((HV, T, NCH, LANES), F32),
            pltpu.VMEM((HV, T, NCH, LANES), F32),
            pltpu.VMEM((HV, T, LANES), F32),
            pltpu.VMEM((HV, MODES, LANES), F32),
            pltpu.VMEM((HV, MODES * NCH, LANES), F32),
            pltpu.VMEM((HV, MODES * NCH, LANES), F32),
            pltpu.VMEM((HV, ROWS, LANES), F32),
            pltpu.VMEM((ROWS, CHL), BF16),
            pltpu.VMEM((ZH, Y, ROWS, CHL), BF16),
            pltpu.VMEM((N_TP, CHL, FEAT), BF16),
            pltpu.VMEM((ROWS, FEAT), F32),
            pltpu.VMEM((2, MODES, CHL), F32),
            pltpu.VMEM((ZL, MODES, CHL), F32),
            pltpu.VMEM((X, MODES, CHL), F32),
            dma((5, 2, PIECES)), dma((5, 2, PIECES)),
            dma((5, 2, PIECES)), dma((5, 2, PIECES)),
            dma((ZH, Y)), dma((ZH, Y)),
            dma((N_TP - 1,)), dma((N_TP - 1,)),
            dma((ZL - 1,)), dma((ZL - 1,)),
            dma((X - 1,)), dma((X - 1,)),
            dma((1,)), dma((1,)),
            dma((ZL + X - 1,)), dma((ZL + X - 1,)),
            dma((2,)),
        ],
        compiler_params=pltpu.CompilerParams(
            collective_id=0, has_side_effects=True, vmem_limit_bytes=56 * 1024 * 1024
        ),
        name="hyena",
    )(
        tokens,
        norm_gain.reshape(D // LANES, LANES),
        w_in.transpose(1, 0, 2),
        w_short,
        residues.T,
        decays.T,
        direct.reshape(1, CHL),
        w_out,
    )


def solution(mesh):
    placed = (
        P("ctx", "tp"),
        P(),
        P(None, None, "tp"),
        P(None, None, "tp"),
        P("tp", None),
        P("tp", None),
        P("tp"),
        P("tp", None),
    )
    return jax.shard_map(local, mesh=mesh, in_specs=placed, out_specs=P("ctx", "tp"), check_vma=False)
```

```python
import jax
import jax.numpy as jnp
from jax import lax
from jax.experimental import pallas as pl
from jax.experimental.pallas import tpu as pltpu
from jax.sharding import PartitionSpec as P

MESH = pl.DeviceIdType.MESH
F32 = jnp.float32
BF16 = jnp.bfloat16

X, ZL, CORES = 4, 4, 2
ZH, Y = 2, 4
N_CTX = X * ZL * CORES
N_TP = ZH * Y
ROWS = 512
FEAT = 512
D = 4096
CHL = 256
MODES = 16
PIECES = 4
PROWS = ROWS // PIECES
HALF = PROWS // 2
HALO = 16
WINDOW = 2
EXT = ROWS + HALO
T = 16
NCH = ROWS // T
LANES = 128
HV = CHL // LANES


def remote(src, dst, send, recv, device):
    return pltpu.make_async_remote_copy(
        src_ref=src, dst_ref=dst, send_sem=send, recv_sem=recv, device_id=device, device_id_type=MESH
    )


def kernel(
    tok, gain, w_in, w_short, res, dec, direct, w_out, out,
    xg, halo, wv, xs, ssq, acc, pb, qb, xb, yb, ft, ab, eb, sb, pw, gb, own, gg, wo, wt, oacc,
    st_core, st_z, st_x, st_in,
    s1, r1, s2, r2, hs, hr, ws, wr, zs, zr, xsnd, xrcv, cs, cr, es, er, lsem,
):
    ctx = lax.axis_index("ctx")
    tp = lax.axis_index("tp")
    x, zl, core = ctx // (ZL * CORES), (ctx // CORES) % ZL, ctx % CORES
    zh, y = tp // Y, tp % Y

    def at_ctx(xx, zz, cc):
        return ((xx * ZL + zz) * CORES + cc, tp)

    def at_tp(hh, yy):
        return (ctx, hh * Y + yy)

    right, left = at_tp(zh, (y + 1) % Y), at_tp(zh, (y + Y - 1) % Y)
    across = at_tp(1 - zh, y)
    y_dev = [at_tp(zh, (y + b) % Y) for b in range(1, Y)]
    z_dev = [at_ctx(x, (zl + b) % ZL, core) for b in range(1, ZL)]
    x_dev = [at_ctx((x + a) % X, zl, core) for a in range(1, X)]
    other = at_ctx(x, zl, 1 - core)
    after = ((ctx + 1) % N_CTX, tp)
    before = ((ctx + N_CTX - 1) % N_CTX, tp)

    w_load = pltpu.make_async_copy(w_in, wv, lsem.at[0])
    w_load.start()

    barrier = pltpu.get_barrier_semaphore()
    greeted = y_dev + z_dev + x_dev + [across, other, after, before]
    for device in greeted:
        pl.semaphore_signal(barrier, inc=1, device_id=device, device_id_type=MESH)
    pl.semaphore_wait(barrier, len(greeted))

    def rows_of(c, half=None):
        start = ROWS - PROWS * (c + 1)
        if half is None:
            return pl.ds(start, PROWS)
        return pl.ds(start + half * HALF, HALF)

    class Gather:
        def __init__(self, mine, buf, send, recv):
            self.mine, self.buf, self.send, self.recv = mine, buf, send, recv
            self.queue = []

        def held(self, p, s):
            return self.mine if (p, s) == (0, 0) else self.buf.at[p, s]

        def copy(self, kind, p, c):
            if kind == 0:
                src, dst, dev = self.held(p, 0).at[rows_of(c)], self.buf.at[p, 1, rows_of(c)], right
            elif kind == 1:
                src, dst, dev = self.held(p, 0).at[rows_of(c)], self.buf.at[p, 3, rows_of(c)], left
            elif kind == 2:
                src, dst, dev = self.buf.at[p, 1, rows_of(c, 0)], self.buf.at[p, 2, rows_of(c, 0)], right
            elif kind == 3:
                src, dst, dev = self.buf.at[p, 3, rows_of(c, 1)], self.buf.at[p, 2, rows_of(c, 1)], left
            else:
                src, dst, dev = self.mine.at[rows_of(c)], self.buf.at[1, 0, rows_of(c)], across
            return remote(src, dst, self.send.at[kind, p, c], self.recv.at[kind, p, c], dev)

        def push(self, *copies):
            if len(self.queue) >= WINDOW:
                for copy in self.queue[-WINDOW]:
                    copy.wait_send()
            for copy in copies:
                copy.start()
            self.queue.append(copies)

        def cross(self, c):
            if c:
                self.copy(4, 0, c - 1).wait_send()
            self.copy(4, 0, c).start()

        def spread(self, p, c):
            if p == 1:
                self.copy(4, 0, c).wait_recv()
            self.push(self.copy(0, p, c), self.copy(1, p, c))

        def forward(self, p, c):
            self.copy(0, p, c).wait_recv()
            self.copy(1, p, c).wait_recv()
            self.push(self.copy(2, p, c), self.copy(3, p, c))

        def arrive(self, p, c):
            self.copy(2, p, c).wait_recv()
            self.copy(3, p, c).wait_recv()

        def sent(self):
            self.copy(4, 0, PIECES - 1).wait_send()
            for copies in self.queue[-WINDOW:]:
                for copy in copies:
                    copy.wait_send()

    def owner(p, s):
        return (zh + p) % ZH * Y + (y + (0, Y - 1, 2, 1)[s]) % Y

    tokens = Gather(tok, xg, s1, r1)

    def halo_copy(p, s):
        return remote(
            tokens.held(p, s).at[pl.ds(ROWS - HALO, HALO)], halo.at[p, s], hs.at[p, s], hr.at[p, s], after
        )

    chip = x * ZL + zl
    lane0 = pl.multiple_of(core * CHL, CHL)

    wo_rows = pl.ds(pl.multiple_of(chip * HALO, HALO), HALO)
    wo_lanes = pl.ds(lane0, CHL)

    def wo_columns(device):
        return w_out.at[wo_rows, pl.ds(pl.multiple_of(device[1] * FEAT + core * CHL, CHL), CHL)]

    def wo_across(b):
        dst = wt.at[b - 1] if b else wo.at[tp, wo_rows, wo_lanes]
        return remote(wo_columns(at_tp(1 - zh, (y + b) % Y)), dst, ws.at[b], wr.at[b], across)

    def wo_y(b):
        dst = wo.at[tp, wo_rows, wo_lanes]
        return remote(wo_columns(y_dev[b - 1]), dst, ws.at[Y + b - 1], wr.at[Y + b - 1], y_dev[b - 1])

    def wo_relayed(b):
        dst = wo.at[across[1], wo_rows, wo_lanes]
        at = 2 * Y + b - 2
        return remote(wt.at[b - 1], dst, ws.at[at], wr.at[at], y_dev[b - 1])

    def wo_mine():
        return pltpu.make_async_copy(wo_columns((ctx, tp)), wo.at[tp, wo_rows, wo_lanes], lsem.at[1])

    def wo_z(i):
        part = wo.at[:, wo_rows, wo_lanes]
        return remote(part, part, zs.at[i], zr.at[i], z_dev[i])

    def wo_x(i):
        part = wo.at[:, pl.ds(pl.multiple_of(x * ZL * HALO, ZL * HALO), ZL * HALO), wo_lanes]
        return remote(part, part, xsnd.at[i], xrcv.at[i], x_dev[i])

    def wo_core():
        part = wo.at[:, :, wo_lanes]
        return remote(part, part, cs.at[0], cr.at[0], other)

    def project(p, s):
        halo_copy(p, s).wait_recv()
        k = owner(p, s)
        block = tokens.held(p, s)
        scale = jnp.concatenate([gain[pl.ds(4 * k + i, 1), :] for i in range(4)], axis=1)
        head = halo[p, s].astype(F32)
        xs[0:HALO, :] = (head * scale).astype(BF16)
        ssq[0:HALO, :] += sum(jnp.square(head[:, LANES * i:LANES * (i + 1)]) for i in range(4))

        @pl.loop(0, ROWS // 64)
        def _(i):
            at = pl.ds(pl.multiple_of(i * 64, 64), 64)
            to = pl.ds(pl.multiple_of(i * 64 + HALO, HALO), 64)
            values = block[at, :].astype(F32)
            xs[to, :] = (values * scale).astype(BF16)
            ssq[to, :] += sum(jnp.square(values[:, LANES * j:LANES * (j + 1)]) for j in range(4))

        @pl.loop(0, 3)
        def _(g):
            weights = wv[g, pl.ds(pl.multiple_of(k * FEAT, FEAT), FEAT), :]
            acc[g] += jnp.dot(xs[...], weights, preferred_element_type=F32)

    tokens.cross(0)
    tokens.spread(0, 0)
    tokens.spread(0, 1)
    halo_copy(0, 0).start()
    for b in range(Y):
        wo_across(b).start()
    for b in range(1, Y):
        wo_y(b).start()
    wo_mine().start()

    ssq[...] = jnp.zeros_like(ssq)
    acc[...] = jnp.zeros_like(acc)
    rate = dec[...]
    weight = res[...]
    powers = []
    for lag in range(T):
        row = jnp.sum(weight * jnp.exp(-rate * float(lag)), axis=0, keepdims=True)
        if lag == 0:
            row = row + direct[...]
        for h in range(HV):
            ft[h, lag:lag + 1, :] = row[:, LANES * h:LANES * (h + 1)]
    decay1 = jnp.exp(-rate)
    for h in range(HV):
        ab[h] = decay1[:, LANES * h:LANES * (h + 1)]

    @pl.loop(0, NCH)
    def _(n):
        table = res[...] * jnp.exp(-dec[...] * (T * n + 1).astype(F32))
        for h in range(HV):
            pw[h, pl.ds(pl.multiple_of(n * MODES, MODES), MODES), :] = table[:, LANES * h:LANES * (h + 1)]


    tokens.spread(0, 2)
    tokens.forward(0, 0)
    halo_copy(0, 1).start()
    halo_copy(0, 3).start()
    tokens.cross(1)
    w_load.wait()
    project(0, 0)
    tokens.spread(0, 3)
    tokens.forward(0, 1)
    tokens.arrive(0, 0)
    halo_copy(0, 2).start()
    tokens.cross(2)
    tokens.forward(0, 2)
    for b in range(1, Y):
        wo_across(b).wait_recv()
        wo_relayed(b).start()
    tokens.forward(0, 3)
    tokens.spread(1, 0)
    halo_copy(1, 0).start()
    project(0, 1)
    tokens.spread(1, 1)
    tokens.cross(3)
    project(0, 3)
    for c in range(1, PIECES):
        tokens.arrive(0, c)
    project(0, 2)
    tokens.forward(1, 0)
    halo_copy(1, 1).start()
    halo_copy(1, 3).start()
    tokens.spread(1, 2)
    wo_mine().wait()
    wo_across(0).wait_recv()
    for b in range(1, Y):
        wo_y(b).wait_recv()
        wo_relayed(b).wait_recv()
    for i in range(ZL - 1):
        wo_z(i).start()
    tokens.forward(1, 1)
    tokens.arrive(1, 0)
    halo_copy(1, 2).start()
    for i in range(ZL - 1):
        wo_z(i).wait_recv()
    for i in range(X - 1):
        wo_x(i).start()
    tokens.spread(1, 3)
    project(1, 0)
    tokens.forward(1, 2)
    tokens.forward(1, 3)
    project(1, 1)
    project(1, 3)
    for c in range(1, PIECES):
        tokens.arrive(1, c)
    project(1, 2)

    inverse = lax.rsqrt(jnp.sum(ssq[...], axis=1, keepdims=True) * (1.0 / D) + 1e-06)
    row_id = lax.broadcasted_iota(jnp.int32, (EXT, 1), 0)
    inverse = jnp.where((row_id < HALO) & (ctx == 0), 0.0, inverse)
    for g in range(3):
        for h in range(HV):
            pb[g, h] = (acc[g, :, LANES * h:LANES * (h + 1)] * inverse).astype(BF16).astype(F32)

    for h in range(HV):
        lanes = pl.ds(LANES * h, LANES)
        taps = [[w_short[j, pl.ds(g, 1), lanes] for j in range(3)] for g in range(3)]

        def plane(g, t):
            return pb[g, h, pl.ds(HALO + t, NCH, stride=T), :]

        def filtered(t, kept):
            streams, keep = [], []
            for g in range(3):
                now = plane(g, t)
                older, old = kept[2 * g:2 * g + 2]
                streams.append(taps[g][0] * now + taps[g][1] * old + taps[g][2] * older)
                keep += [old, now]
            qb[h, t] = streams[0]
            xb[h, t] = streams[1] * streams[2]
            return tuple(keep)

        lax.fori_loop(0, T, filtered, tuple(plane(g, t) for g in range(3) for t in (-2, -1)), unroll=2)

    group = 4
    for h in range(HV):
        for r0 in range(0, MODES, group):
            factors = [jnp.broadcast_to(ab[h, r:r + 1, :], (NCH, LANES)) for r in range(r0, r0 + group)]

            def step(t, states):
                value = xb[h, t]
                return tuple(f * s + value for f, s in zip(factors, states))

            states = lax.fori_loop(0, T, step, tuple(jnp.zeros((NCH, LANES), F32) for _ in factors), unroll=4)
            for i, s in enumerate(states):
                eb[h, (r0 + i) * NCH:(r0 + i + 1) * NCH, :] = s

    block_end = []
    for h in range(HV):
        chunk_decay = jnp.exp(-dec[:, LANES * h:LANES * (h + 1)] * float(T))

        def scan(n, state):
            sb[h, pl.ds(pl.multiple_of(n * MODES, MODES), MODES), :] = state
            return chunk_decay * state + eb[h, pl.ds(n, MODES, stride=NCH), :]

        block_end.append(lax.fori_loop(0, NCH, scan, jnp.zeros((MODES, LANES), F32), unroll=4))
    mine = jnp.concatenate(block_end, axis=1)

    st_core[0] = mine
    core_copy = remote(st_core.at[0], st_core.at[1], es.at[0], er.at[0], other)
    core_copy.start()
    decay_block = jnp.exp(-dec[...] * float(ROWS))
    decay_chip = jnp.exp(-dec[...] * float(ROWS * CORES))
    decay_line = jnp.exp(-dec[...] * float(ROWS * CORES * ZL))
    core_copy.wait_recv()
    theirs = st_core[1]
    st_z[0] = jnp.where(core == 0, decay_block * mine + theirs, decay_block * theirs + mine)
    z_copies = [
        remote(st_z.at[0], st_z.at[b], es.at[b], er.at[b], z_dev[b - 1]) for b in range(1, ZL)
    ]
    for copy in z_copies:
        copy.start()

    def within(h):
        for t in range(T):
            total = None
            for lag in range(t + 1):
                term = ft[h, lag:lag + 1, :] * xb[h, t - lag]
                total = term if total is None else total + term
            yb[h, t] = total

    for h in range(HV):
        front = res[:, LANES * h:LANES * (h + 1)] * ab[h]

        @pl.loop(0, NCH)
        def _(n):
            at = pl.ds(pl.multiple_of(n * MODES, MODES), MODES)
            sb[h, at, :] = front * sb[h, at, :]

    within(0)
    for copy in z_copies:
        copy.wait_recv()
    line_end = jnp.zeros((MODES, CHL), F32)
    chip_in = jnp.zeros((MODES, CHL), F32)
    for zz in range(ZL):
        for b in range(ZL):
            here = (zl + ZL - b) % ZL == zz
            piece = st_z[b]
            if b == 0:
                chosen = jnp.where(here, piece, 0.0)
            else:
                chosen = jnp.where(here, piece, chosen)
        line_end = decay_chip * line_end + chosen
        chip_in = jnp.where(zz < zl, decay_chip * chip_in + chosen, chip_in)
    st_x[0] = line_end
    x_copies = [
        remote(st_x.at[0], st_x.at[a], es.at[ZL + a - 1], er.at[ZL + a - 1], x_dev[a - 1]) for a in range(1, X)
    ]
    for copy in x_copies:
        copy.start()
    within(1)
    before_chip = jnp.exp(-dec[...] * (ROWS * CORES * zl).astype(F32))
    for copy in x_copies:
        copy.wait_recv()
    for i in range(X - 1):
        wo_x(i).wait_recv()
    wo_core().start()
    line_in = jnp.zeros((MODES, CHL), F32)
    for xx in range(X):
        for a in range(X):
            here = (x + X - a) % X == xx
            piece = st_x[a]
            if a == 0:
                chosen = jnp.where(here, piece, 0.0)
            else:
                chosen = jnp.where(here, piece, chosen)
        line_in = jnp.where(xx < x, decay_line * line_in + chosen, line_in)
    chip_in = chip_in + before_chip * line_in
    carried = jnp.where(core == 0, chip_in, decay_block * chip_in + theirs)

    st_in[...] = carried
    per = NCH // PIECES

    def gate(c):
        n0 = per * (PIECES - 1 - c)
        for h in range(HV):
            lanes = pl.ds(LANES * h, LANES)
            factors, start = [], []
            for r in range(MODES):
                at = pl.ds(n0 * MODES + r, per, stride=MODES)
                factors.append(jnp.broadcast_to(ab[h, r:r + 1, :], (per, LANES)))
                start.append(sb[h, at, :] + pw[h, at, :] * st_in[r:r + 1, lanes])

            def step(t, terms):
                sums = list(terms)
                while len(sums) > 1:
                    sums = [a + b for a, b in zip(sums[::2], sums[1::2])]
                total = yb[h, t, pl.ds(n0, per), :] + sums[0]
                gb[h, pl.ds(n0 * T + t, per, stride=T), :] = qb[h, t, pl.ds(n0, per), :] * total
                return tuple(f * s for f, s in zip(factors, terms))

            lax.fori_loop(0, T, step, tuple(start), unroll=2)
        for h in range(HV):
            own[rows_of(c), LANES * h:LANES * (h + 1)] = gb[h, rows_of(c), :].astype(BF16)

    gates = Gather(own, gg, s2, r2)

    def emit(p, s, first=False, last=False):
        weights = wo[owner(p, s)]
        value = jnp.dot(gates.held(p, s)[...], weights, preferred_element_type=F32)
        if first:
            oacc[...] = value
        elif last:
            out[...] = (oacc[...] + value).astype(BF16)
        else:
            oacc[...] += value

    gate(0)
    gates.cross(0)
    gates.spread(0, 0)
    gate(1)
    gates.spread(0, 1)
    gate(2)
    gate(3)
    gates.spread(0, 2)
    gates.cross(1)
    gates.forward(0, 0)
    wo_core().wait_recv()
    emit(0, 0, first=True)
    gates.spread(0, 3)
    gates.forward(0, 1)
    gates.cross(2)
    gates.forward(0, 2)
    gates.spread(1, 0)
    gates.forward(0, 3)
    gates.cross(3)
    emit(0, 1)
    emit(0, 3)
    gates.spread(1, 1)
    gates.forward(1, 0)
    for c in range(PIECES):
        gates.arrive(0, c)
    gates.spread(1, 2)
    emit(0, 2)
    gates.forward(1, 1)
    gates.spread(1, 3)
    emit(1, 0)
    gates.forward(1, 2)
    gates.forward(1, 3)
    emit(1, 1)
    emit(1, 3)
    for c in range(PIECES):
        gates.arrive(1, c)
    emit(1, 2, last=True)

    tokens.sent()
    gates.sent()
    for p in range(ZH):
        for s in range(Y):
            halo_copy(p, s).wait_send()
    for b in range(Y):
        wo_across(b).wait_send()
    for b in range(1, Y):
        wo_y(b).wait_send()
        wo_relayed(b).wait_send()
    for i in range(ZL - 1):
        wo_z(i).wait_send()
    for i in range(X - 1):
        wo_x(i).wait_send()
    wo_core().wait_send()
    core_copy.wait_send()
    for copy in z_copies + x_copies:
        copy.wait_send()


def local(tokens, norm_gain, w_in, w_short, residues, decays, direct, w_out):
    dma = pltpu.SemaphoreType.DMA
    vmem = pl.BlockSpec(memory_space=pltpu.VMEM)
    hbm = pl.BlockSpec(memory_space=pl.ANY)
    return pl.pallas_call(
        kernel,
        out_shape=pltpu.VMEM((ROWS, FEAT), BF16),
        in_specs=[vmem, vmem, hbm, vmem, vmem, vmem, vmem, hbm],
        out_specs=vmem,
        scratch_shapes=[
            pltpu.VMEM((ZH, Y, ROWS, FEAT), BF16),
            pltpu.VMEM((ZH, Y, HALO, FEAT), BF16),
            pltpu.VMEM((3, D, CHL), BF16),
            pltpu.VMEM((EXT, FEAT), BF16),
            pltpu.VMEM((EXT, LANES), F32),
            pltpu.VMEM((3, EXT, CHL), F32),
            pltpu.VMEM((3, HV, EXT, LANES), F32),
            pltpu.VMEM((HV, T, NCH, LANES), F32),
            pltpu.VMEM((HV, T, NCH, LANES), F32),
            pltpu.VMEM((HV, T, NCH, LANES), F32),
            pltpu.VMEM((HV, T, LANES), F32),
            pltpu.VMEM((HV, MODES, LANES), F32),
            pltpu.VMEM((HV, MODES * NCH, LANES), F32),
            pltpu.VMEM((HV, MODES * NCH, LANES), F32),
            pltpu.VMEM((HV, MODES * NCH, LANES), F32),
            pltpu.VMEM((HV, ROWS, LANES), F32),
            pltpu.VMEM((ROWS, CHL), BF16),
            pltpu.VMEM((ZH, Y, ROWS, CHL), BF16),
            pltpu.VMEM((N_TP, CHL, FEAT), BF16),
            pltpu.VMEM((Y - 1, HALO, CHL), BF16),
            pltpu.VMEM((ROWS, FEAT), F32),
            pltpu.VMEM((2, MODES, CHL), F32),
            pltpu.VMEM((ZL, MODES, CHL), F32),
            pltpu.VMEM((X, MODES, CHL), F32),
            pltpu.VMEM((MODES, CHL), F32),
            dma((5, 2, PIECES)), dma((5, 2, PIECES)),
            dma((5, 2, PIECES)), dma((5, 2, PIECES)),
            dma((ZH, Y)), dma((ZH, Y)),
            dma((3 * Y - 2,)), dma((3 * Y - 2,)),
            dma((ZL - 1,)), dma((ZL - 1,)),
            dma((X - 1,)), dma((X - 1,)),
            dma((1,)), dma((1,)),
            dma((ZL + X - 1,)), dma((ZL + X - 1,)),
            dma((2,)),
        ],
        compiler_params=pltpu.CompilerParams(
            collective_id=0, has_side_effects=True, vmem_limit_bytes=56 * 1024 * 1024
        ),
        name="hyena",
    )(
        tokens,
        norm_gain.reshape(D // LANES, LANES),
        w_in.transpose(1, 0, 2),
        w_short,
        residues.T,
        decays.T,
        direct.reshape(1, CHL),
        w_out,
    )


def solution(mesh):
    placed = (
        P("ctx", "tp"),
        P(),
        P(None, None, "tp"),
        P(None, None, "tp"),
        P("tp", None),
        P("tp", None),
        P("tp"),
        P("tp", None),
    )
    return jax.shard_map(local, mesh=mesh, in_specs=placed, out_specs=P("ctx", "tp"), check_vma=False)
```

```python
import jax
import jax.numpy as jnp
from jax import lax
from jax.experimental import pallas as pl
from jax.experimental.pallas import tpu as pltpu
from jax.sharding import PartitionSpec as P

MESH = pl.DeviceIdType.MESH
F32 = jnp.float32
BF16 = jnp.bfloat16

X, ZL, CORES = 4, 4, 2
ZH, Y = 2, 4
N_CTX = X * ZL * CORES
N_TP = ZH * Y
ROWS = 512
FEAT = 512
D = 4096
CHL = 256
MODES = 16
GATED = 4
HALO = 16
EXT = ROWS + HALO
T = 16
NCH = ROWS // T
LANES = 128
HV = CHL // LANES


def remote(src, dst, send, recv, device):
    return pltpu.make_async_remote_copy(
        src_ref=src, dst_ref=dst, send_sem=send, recv_sem=recv, device_id=device, device_id_type=MESH
    )


def kernel(
    tok_in, gain_in, w_in, taps_in, res_in, dec_in, direct_in, w_out, out,
    gain, w_short, res, dec, direct,
    xg, halo, wv, xs, ssq, acc, pb, qb, xb, yb, ft, ab, eb, sb, pw, gb, own, gg, wo, wt, oacc,
    st_core, st_z, st_x, st_in,
    s1, r1, s2, r2, hs, hr, ws, wr, zs, zr, xsnd, xrcv, cs, cr, es, er, lsem,
):
    ctx = lax.axis_index("ctx")
    tp = lax.axis_index("tp")
    x, zl, core = ctx // (ZL * CORES), (ctx // CORES) % ZL, ctx % CORES
    zh, y = tp // Y, tp % Y

    def at_ctx(xx, zz, cc):
        return ((xx * ZL + zz) * CORES + cc, tp)

    def at_tp(hh, yy):
        return (ctx, hh * Y + yy)

    right, left = at_tp(zh, (y + 1) % Y), at_tp(zh, (y + Y - 1) % Y)
    across = at_tp(1 - zh, y)
    y_dev = [at_tp(zh, (y + b) % Y) for b in range(1, Y)]
    z_dev = [at_ctx(x, (zl + b) % ZL, core) for b in range(1, ZL)]
    x_dev = [at_ctx((x + a) % X, zl, core) for a in range(1, X)]
    other = at_ctx(x, zl, 1 - core)
    after = ((ctx + 1) % N_CTX, tp)
    before = ((ctx + N_CTX - 1) % N_CTX, tp)

    barrier = pltpu.get_barrier_semaphore()
    greeted = y_dev + z_dev + x_dev + [across, other, after, before]
    for device in greeted:
        pl.semaphore_signal(barrier, inc=1, device_id=device, device_id_type=MESH)
    small = [(gain_in, gain), (taps_in, w_short), (res_in, res), (dec_in, dec), (direct_in, direct)]
    tok = xg.at[0, 0]
    loads = [pltpu.make_async_copy(a, b, lsem.at[2 + i]) for i, (a, b) in enumerate([(tok_in, tok)] + small)]
    for load in loads:
        load.start()
    w_load = pltpu.make_async_copy(w_in, wv, lsem.at[0])
    w_load.start()
    for load in loads:
        load.wait()
    pl.semaphore_wait(barrier, len(greeted))

    class Gather:
        def __init__(self, mine, buf, send, recv, pieces, window, crossing):
            self.mine, self.buf, self.send, self.recv = mine, buf, send, recv
            self.pieces, self.window, self.crossing = pieces, window, crossing
            self.queue = []

        def rows(self, c, half=None):
            size = ROWS // self.pieces
            start = ROWS - size * (c + 1)
            return pl.ds(start, size) if half is None else pl.ds(start + half * (size // 2), size // 2)

        def held(self, p, s):
            return self.mine if (p, s) == (0, 0) else self.buf.at[p, s]

        def copy(self, kind, p, c):
            if kind == 0:
                src, dst, dev = self.held(p, 0).at[self.rows(c)], self.buf.at[p, 1, self.rows(c)], right
            elif kind == 1:
                src, dst, dev = self.held(p, 0).at[self.rows(c)], self.buf.at[p, 3, self.rows(c)], left
            elif kind == 2:
                src, dst, dev = self.buf.at[p, 1, self.rows(c, 0)], self.buf.at[p, 2, self.rows(c, 0)], right
            elif kind == 3:
                src, dst, dev = self.buf.at[p, 3, self.rows(c, 1)], self.buf.at[p, 2, self.rows(c, 1)], left
            else:
                src, dst, dev = self.mine.at[self.rows(c)], self.buf.at[1, 0, self.rows(c)], across
            return remote(src, dst, self.send.at[kind, p, c], self.recv.at[kind, p, c], dev)

        def push(self, *copies):
            if len(self.queue) >= self.window:
                for copy in self.queue[-self.window]:
                    copy.wait_send()
            for copy in copies:
                copy.start()
            self.queue.append(copies)

        def cross(self, c):
            if c >= self.crossing:
                self.copy(4, 0, c - self.crossing).wait_send()
            self.copy(4, 0, c).start()

        def spread(self, p, c):
            if p == 1:
                self.copy(4, 0, c).wait_recv()
            self.push(self.copy(0, p, c), self.copy(1, p, c))

        def forward(self, p, c):
            self.copy(0, p, c).wait_recv()
            self.copy(1, p, c).wait_recv()
            self.push(self.copy(2, p, c), self.copy(3, p, c))

        def arrive(self, p, c):
            self.copy(2, p, c).wait_recv()
            self.copy(3, p, c).wait_recv()

        def sent(self):
            for c in range(self.pieces - self.crossing, self.pieces):
                self.copy(4, 0, c).wait_send()
            for copies in self.queue[-self.window:]:
                for copy in copies:
                    copy.wait_send()

    def owner(p, s):
        return (zh + p) % ZH * Y + (y + (0, Y - 1, 2, 1)[s]) % Y

    tokens = Gather(tok, xg, s1, r1, 4, 2, 1)

    def halo_copy(p, s):
        return remote(
            tokens.held(p, s).at[pl.ds(ROWS - HALO, HALO)], halo.at[p, s], hs.at[p, s], hr.at[p, s], after
        )

    chip = x * ZL + zl

    wo_rows = pl.ds(pl.multiple_of(chip * HALO, HALO), HALO)

    def wo_columns(device):
        return w_out.at[wo_rows, pl.ds(pl.multiple_of(device[1] * FEAT + core * CHL, CHL), CHL)]

    def wo_across(b):
        dst = wt.at[b - 1] if b else wo.at[core, chip, tp]
        return remote(wo_columns(at_tp(1 - zh, (y + b) % Y)), dst, ws.at[b], wr.at[b], across)

    def wo_y(b):
        dst = wo.at[core, chip, tp]
        return remote(wo_columns(y_dev[b - 1]), dst, ws.at[Y + b - 1], wr.at[Y + b - 1], y_dev[b - 1])

    def wo_relayed(b):
        dst = wo.at[core, chip, across[1]]
        at = 2 * Y + b - 2
        return remote(wt.at[b - 1], dst, ws.at[at], wr.at[at], y_dev[b - 1])

    def wo_mine():
        return pltpu.make_async_copy(wo_columns((ctx, tp)), wo.at[core, chip, tp], lsem.at[1])

    def groups(part):
        return pl.ds(part * (N_TP // 2), N_TP // 2)

    def wo_z(part):
        block = wo.at[core, chip, groups(part)]
        return [remote(block, block, zs.at[part, i], zr.at[part, i], z_dev[i]) for i in range(ZL - 1)]

    def wo_x(part):
        block = wo.at[core, pl.ds(x * ZL, ZL), groups(part)]
        return [remote(block, block, xsnd.at[part, i], xrcv.at[part, i], x_dev[i]) for i in range(X - 1)]

    def start(copies):
        for copy in copies:
            copy.start()

    def landed(copies):
        for copy in copies:
            copy.wait_recv()

    def left_here(copies):
        for copy in copies:
            copy.wait_send()

    def wo_core(part):
        block = wo.at[core, :, groups(part)]
        return [remote(block, block, cs.at[part], cr.at[part], other)]

    def project(p, s):
        halo_copy(p, s).wait_recv()
        k = owner(p, s)
        block = tokens.held(p, s)
        scale = jnp.concatenate([gain[pl.ds(4 * k + i, 1), :] for i in range(4)], axis=1)
        head = halo[p, s].astype(F32)
        xs[0:HALO, :] = (head * scale).astype(BF16)
        ssq[0:HALO, :] += sum(jnp.square(head[:, LANES * i:LANES * (i + 1)]) for i in range(4))

        @pl.loop(0, ROWS // 64)
        def _(i):
            at = pl.ds(pl.multiple_of(i * 64, 64), 64)
            to = pl.ds(pl.multiple_of(i * 64 + HALO, HALO), 64)
            values = block[at, :].astype(F32)
            xs[to, :] = (values * scale).astype(BF16)
            ssq[to, :] += sum(jnp.square(values[:, LANES * j:LANES * (j + 1)]) for j in range(4))

        @pl.loop(0, 3)
        def _(g):
            weights = wv[g, pl.ds(pl.multiple_of(k * FEAT, FEAT), FEAT), :]
            acc[g] += jnp.dot(xs[...], weights, preferred_element_type=F32)

    tokens.cross(0)
    tokens.spread(0, 0)
    tokens.spread(0, 1)
    halo_copy(0, 0).start()

    ssq[...] = jnp.zeros_like(ssq)
    acc[...] = jnp.zeros_like(acc)
    rate = dec[...]
    weight = res[...]
    powers = []
    for lag in range(T):
        row = jnp.sum(weight * jnp.exp(-rate * float(lag)), axis=0, keepdims=True)
        if lag == 0:
            row = row + direct[...]
        for h in range(HV):
            ft[h, lag:lag + 1, :] = row[:, LANES * h:LANES * (h + 1)]
    decay1 = jnp.exp(-rate)
    for h in range(HV):
        ab[h] = decay1[:, LANES * h:LANES * (h + 1)]

    @pl.loop(0, NCH)
    def _(n):
        table = res[...] * jnp.exp(-dec[...] * (T * n + 1).astype(F32))
        for h in range(HV):
            pw[h, pl.ds(pl.multiple_of(n * MODES, MODES), MODES), :] = table[:, LANES * h:LANES * (h + 1)]


    tokens.spread(0, 2)
    tokens.forward(0, 0)
    halo_copy(0, 1).start()
    halo_copy(0, 3).start()
    tokens.cross(1)
    w_load.wait()
    project(0, 0)
    tokens.spread(0, 3)
    tokens.forward(0, 1)
    tokens.arrive(0, 0)
    halo_copy(0, 2).start()
    tokens.cross(2)
    tokens.forward(0, 2)
    tokens.forward(0, 3)
    tokens.spread(1, 0)
    halo_copy(1, 0).start()
    project(0, 1)
    tokens.spread(1, 1)
    tokens.cross(3)
    project(0, 3)
    for c in range(1, 4):
        tokens.arrive(0, c)
    project(0, 2)
    tokens.forward(1, 0)
    halo_copy(1, 1).start()
    halo_copy(1, 3).start()
    tokens.spread(1, 2)
    tokens.forward(1, 1)
    tokens.arrive(1, 0)
    halo_copy(1, 2).start()
    for b in range(Y):
        wo_across(b).start()
    for b in range(1, Y):
        wo_y(b).start()
    wo_mine().start()
    tokens.spread(1, 3)
    project(1, 0)
    tokens.forward(1, 2)
    for b in range(1, Y):
        wo_across(b).wait_recv()
        wo_relayed(b).start()
    tokens.forward(1, 3)
    project(1, 1)
    project(1, 3)
    wo_mine().wait()
    wo_across(0).wait_recv()
    for b in range(1, Y):
        wo_y(b).wait_recv()
        wo_relayed(b).wait_recv()
    start(wo_z(0) + wo_z(1))
    for c in range(1, 4):
        tokens.arrive(1, c)
    project(1, 2)

    inverse = lax.rsqrt(jnp.sum(ssq[...], axis=1, keepdims=True) * (1.0 / D) + 1e-06)
    row_id = lax.broadcasted_iota(jnp.int32, (EXT, 1), 0)
    inverse = jnp.where((row_id < HALO) & (ctx == 0), 0.0, inverse)
    for g in range(3):
        for h in range(HV):
            pb[g, h] = (acc[g, :, LANES * h:LANES * (h + 1)] * inverse).astype(BF16).astype(F32)

    for h in range(HV):
        lanes = pl.ds(LANES * h, LANES)
        taps = [[w_short[j, pl.ds(g, 1), lanes] for j in range(3)] for g in range(3)]

        def plane(g, t):
            return pb[g, h, pl.ds(HALO + t, NCH, stride=T), :]

        def filtered(t, kept):
            streams, keep = [], []
            for g in range(3):
                now = plane(g, t)
                older, old = kept[2 * g:2 * g + 2]
                streams.append(taps[g][0] * now + taps[g][1] * old + taps[g][2] * older)
                keep += [old, now]
            qb[h, t] = streams[0]
            xb[h, t] = streams[1] * streams[2]
            return tuple(keep)

        lax.fori_loop(0, T, filtered, tuple(plane(g, t) for g in range(3) for t in (-2, -1)), unroll=2)

    group = 4
    for h in range(HV):
        for r0 in range(0, MODES, group):
            factors = [jnp.broadcast_to(ab[h, r:r + 1, :], (NCH, LANES)) for r in range(r0, r0 + group)]

            def step(t, states):
                value = xb[h, t]
                return tuple(f * s + value for f, s in zip(factors, states))

            states = lax.fori_loop(0, T, step, tuple(jnp.zeros((NCH, LANES), F32) for _ in factors), unroll=4)
            for i, s in enumerate(states):
                eb[h, (r0 + i) * NCH:(r0 + i + 1) * NCH, :] = s

    block_end = []
    for h in range(HV):
        chunk_decay = jnp.exp(-dec[:, LANES * h:LANES * (h + 1)] * float(T))

        def scan(n, state):
            sb[h, pl.ds(pl.multiple_of(n * MODES, MODES), MODES), :] = state
            return chunk_decay * state + eb[h, pl.ds(n, MODES, stride=NCH), :]

        block_end.append(lax.fori_loop(0, NCH, scan, jnp.zeros((MODES, LANES), F32), unroll=4))
    mine = jnp.concatenate(block_end, axis=1)

    st_core[0] = mine
    core_copy = remote(st_core.at[0], st_core.at[1], es.at[0], er.at[0], other)
    core_copy.start()
    decay_block = jnp.exp(-dec[...] * float(ROWS))
    decay_chip = jnp.exp(-dec[...] * float(ROWS * CORES))
    decay_line = jnp.exp(-dec[...] * float(ROWS * CORES * ZL))
    core_copy.wait_recv()
    theirs = st_core[1]
    st_z[0] = jnp.where(core == 0, decay_block * mine + theirs, decay_block * theirs + mine)
    z_copies = [
        remote(st_z.at[0], st_z.at[b], es.at[b], er.at[b], z_dev[b - 1]) for b in range(1, ZL)
    ]
    for copy in z_copies:
        copy.start()

    def within(h):
        for t in range(T):
            total = None
            for lag in range(t + 1):
                term = ft[h, lag:lag + 1, :] * xb[h, t - lag]
                total = term if total is None else total + term
            yb[h, t] = total

    for h in range(HV):
        front = res[:, LANES * h:LANES * (h + 1)] * ab[h]

        @pl.loop(0, NCH)
        def _(n):
            at = pl.ds(pl.multiple_of(n * MODES, MODES), MODES)
            sb[h, at, :] = front * sb[h, at, :]

    within(0)
    for copy in z_copies:
        copy.wait_recv()
    line_end = jnp.zeros((MODES, CHL), F32)
    chip_in = jnp.zeros((MODES, CHL), F32)
    for zz in range(ZL):
        for b in range(ZL):
            here = (zl + ZL - b) % ZL == zz
            piece = st_z[b]
            if b == 0:
                chosen = jnp.where(here, piece, 0.0)
            else:
                chosen = jnp.where(here, piece, chosen)
        line_end = decay_chip * line_end + chosen
        chip_in = jnp.where(zz < zl, decay_chip * chip_in + chosen, chip_in)
    st_x[0] = line_end
    x_copies = [
        remote(st_x.at[0], st_x.at[a], es.at[ZL + a - 1], er.at[ZL + a - 1], x_dev[a - 1]) for a in range(1, X)
    ]
    for copy in x_copies:
        copy.start()
    within(1)
    before_chip = jnp.exp(-dec[...] * (ROWS * CORES * zl).astype(F32))
    for copy in x_copies:
        copy.wait_recv()
    landed(wo_z(0) + wo_z(1))
    start(wo_x(0) + wo_x(1))
    line_in = jnp.zeros((MODES, CHL), F32)
    for xx in range(X):
        for a in range(X):
            here = (x + X - a) % X == xx
            piece = st_x[a]
            if a == 0:
                chosen = jnp.where(here, piece, 0.0)
            else:
                chosen = jnp.where(here, piece, chosen)
        line_in = jnp.where(xx < x, decay_line * line_in + chosen, line_in)
    chip_in = chip_in + before_chip * line_in
    carried = jnp.where(core == 0, chip_in, decay_block * chip_in + theirs)

    st_in[...] = carried
    per = NCH // GATED
    span = ROWS // GATED

    def gate(c):
        n0 = per * (GATED - 1 - c)
        for h in range(HV):
            lanes = pl.ds(LANES * h, LANES)
            factors, terms0 = [], []
            for r in range(MODES):
                at = pl.ds(n0 * MODES + r, per, stride=MODES)
                factors.append(jnp.broadcast_to(ab[h, r:r + 1, :], (per, LANES)))
                terms0.append(sb[h, at, :] + pw[h, at, :] * st_in[r:r + 1, lanes])

            def step(t, terms):
                sums = list(terms)
                while len(sums) > 1:
                    sums = [a + b for a, b in zip(sums[::2], sums[1::2])]
                total = yb[h, t, pl.ds(n0, per), :] + sums[0]
                gb[h, pl.ds(n0 * T + t, per, stride=T), :] = qb[h, t, pl.ds(n0, per), :] * total
                return tuple(f * s for f, s in zip(factors, terms))

            lax.fori_loop(0, T, step, tuple(terms0), unroll=2)
        for h in range(HV):
            at = pl.ds(ROWS - span * (c + 1), span)
            own[at, LANES * h:LANES * (h + 1)] = gb[h, at, :].astype(BF16)

    gates = Gather(own, gg, s2, r2, 4, 4, 1)

    def emit(p, s, first=False, last=False):
        k = owner(p, s)
        block = gates.held(p, s)[...]
        for half in range(CORES):
            weights = wo[half, :, k].reshape(CHL, CHL)
            value = jnp.dot(block, weights, preferred_element_type=F32)
            lanes = slice(CHL * half, CHL * (half + 1))
            if first:
                oacc[:, lanes] = value
            elif last:
                out[:, lanes] = (oacc[:, lanes] + value).astype(BF16)
            else:
                oacc[:, lanes] += value

    gate(0)
    gates.cross(0)
    gates.spread(0, 0)
    gate(1)
    gates.spread(0, 1)
    gate(2)
    gate(3)
    gates.spread(0, 2)
    gates.cross(1)
    gates.forward(0, 0)
    gates.spread(0, 3)
    gates.forward(0, 1)
    gates.cross(2)
    gates.forward(0, 2)
    gates.spread(1, 0)
    gates.forward(0, 3)
    gates.cross(3)
    gates.spread(1, 1)
    gates.forward(1, 0)
    landed(wo_x(0) + wo_x(1))
    start(wo_core(0) + wo_core(1))
    for c in range(4):
        gates.arrive(0, c)
    gates.spread(1, 2)
    landed(wo_core(0) + wo_core(1))
    emit(0, 0, first=True)
    gates.forward(1, 1)
    emit(0, 1)
    emit(0, 3)
    gates.spread(1, 3)
    emit(0, 2)
    emit(1, 0)
    gates.forward(1, 2)
    gates.forward(1, 3)
    emit(1, 1)
    emit(1, 3)
    for c in range(4):
        gates.arrive(1, c)
    emit(1, 2, last=True)

    tokens.sent()
    gates.sent()
    for p in range(ZH):
        for s in range(Y):
            halo_copy(p, s).wait_send()
    for b in range(Y):
        wo_across(b).wait_send()
    for b in range(1, Y):
        wo_y(b).wait_send()
        wo_relayed(b).wait_send()
    for part in range(2):
        left_here(wo_z(part) + wo_x(part) + wo_core(part))
    core_copy.wait_send()
    for copy in z_copies + x_copies:
        copy.wait_send()


def local(tokens, norm_gain, w_in, w_short, residues, decays, direct, w_out):
    dma = pltpu.SemaphoreType.DMA
    vmem = pl.BlockSpec(memory_space=pltpu.VMEM)
    hbm = pl.BlockSpec(memory_space=pl.ANY)
    return pl.pallas_call(
        kernel,
        out_shape=pltpu.VMEM((ROWS, FEAT), BF16),
        in_specs=[hbm] * 8,
        out_specs=vmem,
        scratch_shapes=[
            pltpu.VMEM((D // LANES, LANES), F32),
            pltpu.VMEM((3, 3, CHL), F32),
            pltpu.VMEM((MODES, CHL), F32),
            pltpu.VMEM((MODES, CHL), F32),
            pltpu.VMEM((1, CHL), F32),
            pltpu.VMEM((ZH, Y, ROWS, FEAT), BF16),
            pltpu.VMEM((ZH, Y, HALO, FEAT), BF16),
            pltpu.VMEM((3, D, CHL), BF16),
            pltpu.VMEM((EXT, FEAT), BF16),
            pltpu.VMEM((EXT, LANES), F32),
            pltpu.VMEM((3, EXT, CHL), F32),
            pltpu.VMEM((3, HV, EXT, LANES), F32),
            pltpu.VMEM((HV, T, NCH, LANES), F32),
            pltpu.VMEM((HV, T, NCH, LANES), F32),
            pltpu.VMEM((HV, T, NCH, LANES), F32),
            pltpu.VMEM((HV, T, LANES), F32),
            pltpu.VMEM((HV, MODES, LANES), F32),
            pltpu.VMEM((HV, MODES * NCH, LANES), F32),
            pltpu.VMEM((HV, MODES * NCH, LANES), F32),
            pltpu.VMEM((HV, MODES * NCH, LANES), F32),
            pltpu.VMEM((HV, ROWS, LANES), F32),
            pltpu.VMEM((ROWS, CHL), BF16),
            pltpu.VMEM((ZH, Y, ROWS, CHL), BF16),
            pltpu.VMEM((CORES, X * ZL, N_TP, HALO, CHL), BF16),
            pltpu.VMEM((Y - 1, HALO, CHL), BF16),
            pltpu.VMEM((ROWS, FEAT), F32),
            pltpu.VMEM((2, MODES, CHL), F32),
            pltpu.VMEM((ZL, MODES, CHL), F32),
            pltpu.VMEM((X, MODES, CHL), F32),
            pltpu.VMEM((MODES, CHL), F32),
            dma((5, 2, 4)), dma((5, 2, 4)),
            dma((5, 2, 4)), dma((5, 2, 4)),
            dma((ZH, Y)), dma((ZH, Y)),
            dma((3 * Y - 2,)), dma((3 * Y - 2,)),
            dma((2, ZL - 1)), dma((2, ZL - 1)),
            dma((2, X - 1)), dma((2, X - 1)),
            dma((2,)), dma((2,)),
            dma((ZL + X - 1,)), dma((ZL + X - 1,)),
            dma((8,)),
        ],
        compiler_params=pltpu.CompilerParams(
            collective_id=0, has_side_effects=True, vmem_limit_bytes=56 * 1024 * 1024
        ),
        name="hyena",
    )(
        tokens,
        norm_gain.reshape(D // LANES, LANES),
        w_in.transpose(1, 0, 2),
        w_short,
        residues.T,
        decays.T,
        direct.reshape(1, CHL),
        w_out,
    )


def solution(mesh):
    placed = (
        P("ctx", "tp"),
        P(),
        P(None, None, "tp"),
        P(None, None, "tp"),
        P("tp", None),
        P("tp", None),
        P("tp"),
        P("tp", None),
    )
    return jax.shard_map(local, mesh=mesh, in_specs=placed, out_specs=P("ctx", "tp"), check_vma=False)
```

```python
import jax
import jax.numpy as jnp
from jax import lax
from jax.experimental import pallas as pl
from jax.experimental.pallas import tpu as pltpu
from jax.sharding import PartitionSpec as P

MESH = pl.DeviceIdType.MESH
F32 = jnp.float32
BF16 = jnp.bfloat16

X, ZL, CORES = 4, 4, 2
ZH, Y = 2, 4
N_CTX = X * ZL * CORES
N_TP = ZH * Y
ROWS = 512
FEAT = 512
D = 4096
CHL = 256
MODES = 16
GATED = 4
HALO = 16
EXT = ROWS + HALO
T = 16
NCH = ROWS // T
LANES = 128
HV = CHL // LANES


def remote(src, dst, send, recv, device):
    return pltpu.make_async_remote_copy(
        src_ref=src, dst_ref=dst, send_sem=send, recv_sem=recv, device_id=device, device_id_type=MESH
    )


def kernel(
    tok_in, gain_in, w_in, taps_in, res_in, dec_in, direct_in, w_out, out,
    gain, w_short, res, dec, direct,
    xg, halo, wv, xs, ssq, acc, pb, qb, xb, yb, ft, ab, eb, sb, pw, gb, own, gg, wo, wt, oacc,
    st_core, st_z, st_x, st_in,
    s1, r1, s2, r2, hs, hr, ws, wr, zs, zr, xsnd, xrcv, cs, cr, es, er, lsem,
):
    ctx = lax.axis_index("ctx")
    tp = lax.axis_index("tp")
    x, zl, core = ctx // (ZL * CORES), (ctx // CORES) % ZL, ctx % CORES
    zh, y = tp // Y, tp % Y

    def at_ctx(xx, zz, cc):
        return ((xx * ZL + zz) * CORES + cc, tp)

    def at_tp(hh, yy):
        return (ctx, hh * Y + yy)

    right, left = at_tp(zh, (y + 1) % Y), at_tp(zh, (y + Y - 1) % Y)
    across = at_tp(1 - zh, y)
    y_dev = [at_tp(zh, (y + b) % Y) for b in range(1, Y)]
    z_dev = [at_ctx(x, (zl + b) % ZL, core) for b in range(1, ZL)]
    x_dev = [at_ctx((x + a) % X, zl, core) for a in range(1, X)]
    other = at_ctx(x, zl, 1 - core)
    after = ((ctx + 1) % N_CTX, tp)
    before = ((ctx + N_CTX - 1) % N_CTX, tp)

    barrier = pltpu.get_barrier_semaphore()
    greeted = [across] + z_dev + x_dev + y_dev + [before, after, other]
    for device in greeted:
        pl.semaphore_signal(barrier, inc=1, device_id=device, device_id_type=MESH)
    small = [(gain_in, gain), (taps_in, w_short), (res_in, res), (dec_in, dec), (direct_in, direct)]
    tok = xg.at[0, 0]
    loads = [pltpu.make_async_copy(a, b, lsem.at[2 + i]) for i, (a, b) in enumerate([(tok_in, tok)] + small)]
    for load in loads:
        load.start()
    w_load = pltpu.make_async_copy(w_in, wv, lsem.at[0])
    w_load.start()
    for load in loads:
        load.wait()
    pl.semaphore_wait(barrier, len(greeted))

    class Gather:
        def __init__(self, mine, buf, send, recv, pieces, window, crossing, direct=False):
            self.mine, self.buf, self.send, self.recv = mine, buf, send, recv
            self.pieces, self.window, self.crossing = pieces, window, crossing
            self.queue = []
            self.direct = direct

        def straight(self, p, c):
            return self.direct and (p, c) == (1, self.pieces - 1)

        def rows(self, c, half=None):
            size = ROWS // self.pieces
            start = ROWS - size * (c + 1)
            return pl.ds(start, size) if half is None else pl.ds(start + half * (size // 2), size // 2)

        def held(self, p, s):
            return self.mine if (p, s) == (0, 0) else self.buf.at[p, s]

        def copy(self, kind, p, c):
            if kind == 0:
                src, dst, dev = self.held(p, 0).at[self.rows(c)], self.buf.at[p, 1, self.rows(c)], right
            elif kind == 1:
                src, dst, dev = self.held(p, 0).at[self.rows(c)], self.buf.at[p, 3, self.rows(c)], left
            elif kind == 2:
                src, dst, dev = self.buf.at[p, 1, self.rows(c, 0)], self.buf.at[p, 2, self.rows(c, 0)], right
            elif kind == 3:
                src, dst, dev = self.buf.at[p, 3, self.rows(c, 1)], self.buf.at[p, 2, self.rows(c, 1)], left
            elif kind == 5:
                src, dst, dev = self.held(p, 0).at[self.rows(c)], self.buf.at[p, 2, self.rows(c)], y_dev[1]
            else:
                src, dst, dev = self.mine.at[self.rows(c)], self.buf.at[1, 0, self.rows(c)], across
            return remote(src, dst, self.send.at[kind, p, c], self.recv.at[kind, p, c], dev)

        def push(self, *copies):
            if len(self.queue) >= self.window:
                for copy in self.queue[-self.window]:
                    copy.wait_send()
            for copy in copies:
                copy.start()
            self.queue.append(copies)

        def cross(self, c):
            if c >= self.crossing:
                self.copy(4, 0, c - self.crossing).wait_send()
            self.copy(4, 0, c).start()

        def spread(self, p, c):
            if p == 1:
                self.copy(4, 0, c).wait_recv()
            more = [self.copy(5, p, c)] if self.straight(p, c) else []
            self.push(self.copy(0, p, c), self.copy(1, p, c), *more)

        def forward(self, p, c):
            self.copy(0, p, c).wait_recv()
            self.copy(1, p, c).wait_recv()
            if not self.straight(p, c):
                self.push(self.copy(2, p, c), self.copy(3, p, c))

        def arrive(self, p, c):
            for kind in (5,) if self.straight(p, c) else (2, 3):
                self.copy(kind, p, c).wait_recv()

        def sent(self):
            for c in range(self.pieces - self.crossing, self.pieces):
                self.copy(4, 0, c).wait_send()
            for copies in self.queue[-self.window:]:
                for copy in copies:
                    copy.wait_send()

    def owner(p, s):
        return (zh + p) % ZH * Y + (y + (0, Y - 1, 2, 1)[s]) % Y

    tokens = Gather(tok, xg, s1, r1, 4, 2, 1)

    def halo_copy(p, s):
        return remote(
            tokens.held(p, s).at[pl.ds(ROWS - HALO, HALO)], halo.at[p, s], hs.at[p, s], hr.at[p, s], after
        )

    chip = x * ZL + zl

    wo_rows = pl.ds(pl.multiple_of(chip * HALO, HALO), HALO)

    def wo_columns(device):
        return w_out.at[wo_rows, pl.ds(pl.multiple_of(device[1] * FEAT + core * CHL, CHL), CHL)]

    def wo_across(b):
        dst = wt.at[b - 1] if b else wo.at[core, chip, tp]
        return remote(wo_columns(at_tp(1 - zh, (y + b) % Y)), dst, ws.at[b], wr.at[b], across)

    def wo_y(b):
        dst = wo.at[core, chip, tp]
        return remote(wo_columns(y_dev[b - 1]), dst, ws.at[Y + b - 1], wr.at[Y + b - 1], y_dev[b - 1])

    def wo_relayed(b):
        dst = wo.at[core, chip, across[1]]
        at = 2 * Y + b - 2
        return remote(wt.at[b - 1], dst, ws.at[at], wr.at[at], y_dev[b - 1])

    def wo_mine():
        return pltpu.make_async_copy(wo_columns((ctx, tp)), wo.at[core, chip, tp], lsem.at[1])

    def groups(part):
        return pl.ds(part * (N_TP // 2), N_TP // 2)

    def wo_z(part):
        block = wo.at[core, chip, groups(part)]
        return [remote(block, block, zs.at[part, i], zr.at[part, i], z_dev[i]) for i in range(ZL - 1)]

    def wo_x(part):
        block = wo.at[core, pl.ds(x * ZL, ZL), groups(part)]
        return [remote(block, block, xsnd.at[part, i], xrcv.at[part, i], x_dev[i]) for i in range(X - 1)]

    def start(copies):
        for copy in copies:
            copy.start()

    def landed(copies):
        for copy in copies:
            copy.wait_recv()

    def left_here(copies):
        for copy in copies:
            copy.wait_send()

    def wo_core(part):
        block = wo.at[core, :, groups(part)]
        return [remote(block, block, cs.at[part], cr.at[part], other)]

    def project(p, s, lo=0, hi=EXT):
        k = owner(p, s)
        block = tokens.held(p, s)
        scale = jnp.concatenate([gain[pl.ds(4 * k + i, 1), :] for i in range(4)], axis=1)
        if lo == 0:
            halo_copy(p, s).wait_recv()
            head = halo[p, s].astype(F32)
            xs[0:HALO, :] = (head * scale).astype(BF16)
            ssq[0:HALO, :] += sum(jnp.square(head[:, LANES * i:LANES * (i + 1)]) for i in range(4))

        @pl.loop(max(lo - HALO, 0) // 64, (hi - HALO) // 64)
        def _(i):
            at = pl.ds(pl.multiple_of(i * 64, 64), 64)
            to = pl.ds(pl.multiple_of(i * 64 + HALO, HALO), 64)
            values = block[at, :].astype(F32)
            xs[to, :] = (values * scale).astype(BF16)
            ssq[to, :] += sum(jnp.square(values[:, LANES * j:LANES * (j + 1)]) for j in range(4))

        @pl.loop(0, 3)
        def _(g):
            weights = wv[g, pl.ds(pl.multiple_of(k * FEAT, FEAT), FEAT), :]
            acc[g, lo:hi] += jnp.dot(xs[lo:hi], weights, preferred_element_type=F32)

    tokens.cross(0)
    tokens.spread(0, 0)
    tokens.spread(0, 1)
    halo_copy(0, 0).start()

    ssq[...] = jnp.zeros_like(ssq)
    acc[...] = jnp.zeros_like(acc)
    rate = dec[...]
    weight = res[...]
    powers = []
    for lag in range(T):
        row = jnp.sum(weight * jnp.exp(-rate * float(lag)), axis=0, keepdims=True)
        if lag == 0:
            row = row + direct[...]
        for h in range(HV):
            ft[h, lag:lag + 1, :] = row[:, LANES * h:LANES * (h + 1)]
    decay1 = jnp.exp(-rate)
    for h in range(HV):
        ab[h] = decay1[:, LANES * h:LANES * (h + 1)]

    @pl.loop(0, NCH)
    def _(n):
        table = res[...] * jnp.exp(-dec[...] * (T * n + 1).astype(F32))
        for h in range(HV):
            pw[h, pl.ds(pl.multiple_of(n * MODES, MODES), MODES), :] = table[:, LANES * h:LANES * (h + 1)]


    tokens.spread(0, 2)
    tokens.forward(0, 0)
    halo_copy(0, 1).start()
    halo_copy(0, 3).start()
    tokens.cross(1)
    w_load.wait()
    project(0, 0)
    tokens.spread(0, 3)
    tokens.forward(0, 1)
    tokens.arrive(0, 0)
    halo_copy(0, 2).start()
    tokens.cross(2)
    tokens.forward(0, 2)
    tokens.forward(0, 3)
    tokens.spread(1, 0)
    halo_copy(1, 0).start()
    project(0, 1)
    tokens.spread(1, 1)
    tokens.cross(3)
    project(0, 3)
    for c in range(1, 4):
        tokens.arrive(0, c)
    project(0, 2)
    tokens.forward(1, 0)
    halo_copy(1, 1).start()
    halo_copy(1, 3).start()
    tokens.spread(1, 2)
    tokens.forward(1, 1)
    tokens.arrive(1, 0)
    halo_copy(1, 2).start()
    for b in range(Y):
        wo_across(b).start()
    for b in range(1, Y):
        wo_y(b).start()
    wo_mine().start()
    tokens.spread(1, 3)
    project(1, 0)
    tokens.forward(1, 2)
    for b in range(1, Y):
        wo_across(b).wait_recv()
        wo_relayed(b).start()
    tokens.forward(1, 3)
    project(1, 1)
    project(1, 3)
    wo_mine().wait()
    wo_across(0).wait_recv()
    for b in range(1, Y):
        wo_y(b).wait_recv()
        wo_relayed(b).wait_recv()
    start(wo_z(0) + wo_z(1))
    tokens.arrive(1, 1)
    tokens.arrive(1, 2)
    project(1, 2, HALO + ROWS // 4, EXT)
    tokens.arrive(1, 3)
    project(1, 2, 0, HALO + ROWS // 4)

    inverse = lax.rsqrt(jnp.sum(ssq[...], axis=1, keepdims=True) * (1.0 / D) + 1e-06)
    row_id = lax.broadcasted_iota(jnp.int32, (EXT, 1), 0)
    inverse = jnp.where((row_id < HALO) & (ctx == 0), 0.0, inverse)
    for g in range(3):
        for h in range(HV):
            pb[g, h] = (acc[g, :, LANES * h:LANES * (h + 1)] * inverse).astype(BF16).astype(F32)

    for h in range(HV):
        lanes = pl.ds(LANES * h, LANES)
        taps = [[w_short[j, pl.ds(g, 1), lanes] for j in range(3)] for g in range(3)]

        def plane(g, t):
            return pb[g, h, pl.ds(HALO + t, NCH, stride=T), :]

        def filtered(t, kept):
            streams, keep = [], []
            for g in range(3):
                now = plane(g, t)
                older, old = kept[2 * g:2 * g + 2]
                streams.append(taps[g][0] * now + taps[g][1] * old + taps[g][2] * older)
                keep += [old, now]
            qb[h, t] = streams[0]
            xb[h, t] = streams[1] * streams[2]
            return tuple(keep)

        lax.fori_loop(0, T, filtered, tuple(plane(g, t) for g in range(3) for t in (-2, -1)), unroll=2)

    group = 4
    for h in range(HV):
        for r0 in range(0, MODES, group):
            factors = [jnp.broadcast_to(ab[h, r:r + 1, :], (NCH, LANES)) for r in range(r0, r0 + group)]

            def step(t, states):
                value = xb[h, t]
                return tuple(f * s + value for f, s in zip(factors, states))

            states = lax.fori_loop(0, T, step, tuple(jnp.zeros((NCH, LANES), F32) for _ in factors), unroll=4)
            for i, s in enumerate(states):
                eb[h, (r0 + i) * NCH:(r0 + i + 1) * NCH, :] = s

    block_end = []
    for h in range(HV):
        chunk_decay = jnp.exp(-dec[:, LANES * h:LANES * (h + 1)] * float(T))

        def scan(n, state):
            sb[h, pl.ds(pl.multiple_of(n * MODES, MODES), MODES), :] = state
            return chunk_decay * state + eb[h, pl.ds(n, MODES, stride=NCH), :]

        block_end.append(lax.fori_loop(0, NCH, scan, jnp.zeros((MODES, LANES), F32), unroll=4))
    mine = jnp.concatenate(block_end, axis=1)

    st_core[0] = mine
    core_copy = remote(st_core.at[0], st_core.at[1], es.at[0], er.at[0], other)
    core_copy.start()
    decay_block = jnp.exp(-dec[...] * float(ROWS))
    decay_chip = jnp.exp(-dec[...] * float(ROWS * CORES))
    decay_line = jnp.exp(-dec[...] * float(ROWS * CORES * ZL))
    core_copy.wait_recv()
    theirs = st_core[1]
    st_z[0] = jnp.where(core == 0, decay_block * mine + theirs, decay_block * theirs + mine)
    z_copies = [
        remote(st_z.at[0], st_z.at[b], es.at[b], er.at[b], z_dev[b - 1]) for b in range(1, ZL)
    ]
    for copy in z_copies:
        copy.start()

    def within(h):
        for t in range(T):
            total = None
            for lag in range(t + 1):
                term = ft[h, lag:lag + 1, :] * xb[h, t - lag]
                total = term if total is None else total + term
            yb[h, t] = total

    for h in range(HV):
        front = res[:, LANES * h:LANES * (h + 1)] * ab[h]

        @pl.loop(0, NCH)
        def _(n):
            at = pl.ds(pl.multiple_of(n * MODES, MODES), MODES)
            sb[h, at, :] = front * sb[h, at, :]

    within(0)
    for copy in z_copies:
        copy.wait_recv()
    line_end = jnp.zeros((MODES, CHL), F32)
    chip_in = jnp.zeros((MODES, CHL), F32)
    for zz in range(ZL):
        for b in range(ZL):
            here = (zl + ZL - b) % ZL == zz
            piece = st_z[b]
            if b == 0:
                chosen = jnp.where(here, piece, 0.0)
            else:
                chosen = jnp.where(here, piece, chosen)
        line_end = decay_chip * line_end + chosen
        chip_in = jnp.where(zz < zl, decay_chip * chip_in + chosen, chip_in)
    st_x[0] = line_end
    x_copies = [
        remote(st_x.at[0], st_x.at[a], es.at[ZL + a - 1], er.at[ZL + a - 1], x_dev[a - 1]) for a in range(1, X)
    ]
    for copy in x_copies:
        copy.start()
    within(1)
    before_chip = jnp.exp(-dec[...] * (ROWS * CORES * zl).astype(F32))
    for copy in x_copies:
        copy.wait_recv()
    line_in = jnp.zeros((MODES, CHL), F32)
    for xx in range(X):
        for a in range(X):
            here = (x + X - a) % X == xx
            piece = st_x[a]
            if a == 0:
                chosen = jnp.where(here, piece, 0.0)
            else:
                chosen = jnp.where(here, piece, chosen)
        line_in = jnp.where(xx < x, decay_line * line_in + chosen, line_in)
    chip_in = chip_in + before_chip * line_in
    carried = jnp.where(core == 0, chip_in, decay_block * chip_in + theirs)

    st_in[...] = carried
    per = NCH // GATED
    span = ROWS // GATED

    def gate(c):
        n0 = per * (GATED - 1 - c)
        for h in range(HV):
            lanes = pl.ds(LANES * h, LANES)
            factors, terms0 = [], []
            for r in range(MODES):
                at = pl.ds(n0 * MODES + r, per, stride=MODES)
                factors.append(jnp.broadcast_to(ab[h, r:r + 1, :], (per, LANES)))
                terms0.append(sb[h, at, :] + pw[h, at, :] * st_in[r:r + 1, lanes])

            def step(t, terms):
                sums = list(terms)
                while len(sums) > 1:
                    sums = [a + b for a, b in zip(sums[::2], sums[1::2])]
                total = yb[h, t, pl.ds(n0, per), :] + sums[0]
                gb[h, pl.ds(n0 * T + t, per, stride=T), :] = qb[h, t, pl.ds(n0, per), :] * total
                return tuple(f * s for f, s in zip(factors, terms))

            lax.fori_loop(0, T, step, tuple(terms0), unroll=2)
        for h in range(HV):
            at = pl.ds(ROWS - span * (c + 1), span)
            own[at, LANES * h:LANES * (h + 1)] = gb[h, at, :].astype(BF16)

    gates = Gather(own, gg, s2, r2, 4, 4, 1, direct=True)

    def emit(p, s, first=False, last=False):
        k = owner(p, s)
        block = gates.held(p, s)[...]
        for half in range(CORES):
            weights = wo[half, :, k].reshape(CHL, CHL)
            value = jnp.dot(block, weights, preferred_element_type=F32)
            lanes = slice(CHL * half, CHL * (half + 1))
            if first:
                oacc[:, lanes] = value
            elif last:
                out[:, lanes] = (oacc[:, lanes] + value).astype(BF16)
            else:
                oacc[:, lanes] += value

    gate(0)
    gates.cross(0)
    gates.spread(0, 0)
    landed(wo_z(0) + wo_z(1))
    start(wo_x(0) + wo_x(1))
    gate(1)
    gates.spread(0, 1)
    gate(2)
    gate(3)
    gates.spread(0, 2)
    gates.cross(1)
    gates.forward(0, 0)
    gates.spread(0, 3)
    gates.forward(0, 1)
    gates.cross(2)
    gates.forward(0, 2)
    gates.spread(1, 0)
    gates.forward(0, 3)
    gates.cross(3)
    gates.spread(1, 1)
    gates.forward(1, 0)
    landed(wo_x(0) + wo_x(1))
    start(wo_core(0) + wo_core(1))
    for c in range(4):
        gates.arrive(0, c)
    gates.spread(1, 2)
    landed(wo_core(0) + wo_core(1))
    emit(0, 0, first=True)
    gates.forward(1, 1)
    emit(0, 1)
    emit(0, 3)
    gates.spread(1, 3)
    emit(0, 2)
    emit(1, 0)
    gates.forward(1, 2)
    gates.forward(1, 3)
    emit(1, 1)
    emit(1, 3)
    for c in range(4):
        gates.arrive(1, c)
    emit(1, 2, last=True)

    tokens.sent()
    gates.sent()
    for p in range(ZH):
        for s in range(Y):
            halo_copy(p, s).wait_send()
    for b in range(Y):
        wo_across(b).wait_send()
    for b in range(1, Y):
        wo_y(b).wait_send()
        wo_relayed(b).wait_send()
    for part in range(2):
        left_here(wo_z(part) + wo_x(part) + wo_core(part))
    core_copy.wait_send()
    for copy in z_copies + x_copies:
        copy.wait_send()


def local(tokens, norm_gain, w_in, w_short, residues, decays, direct, w_out):
    dma = pltpu.SemaphoreType.DMA
    vmem = pl.BlockSpec(memory_space=pltpu.VMEM)
    hbm = pl.BlockSpec(memory_space=pl.ANY)
    return pl.pallas_call(
        kernel,
        out_shape=pltpu.VMEM((ROWS, FEAT), BF16),
        in_specs=[hbm] * 8,
        out_specs=vmem,
        scratch_shapes=[
            pltpu.VMEM((D // LANES, LANES), F32),
            pltpu.VMEM((3, 3, CHL), F32),
            pltpu.VMEM((MODES, CHL), F32),
            pltpu.VMEM((MODES, CHL), F32),
            pltpu.VMEM((1, CHL), F32),
            pltpu.VMEM((ZH, Y, ROWS, FEAT), BF16),
            pltpu.VMEM((ZH, Y, HALO, FEAT), BF16),
            pltpu.VMEM((3, D, CHL), BF16),
            pltpu.VMEM((EXT, FEAT), BF16),
            pltpu.VMEM((EXT, LANES), F32),
            pltpu.VMEM((3, EXT, CHL), F32),
            pltpu.VMEM((3, HV, EXT, LANES), F32),
            pltpu.VMEM((HV, T, NCH, LANES), F32),
            pltpu.VMEM((HV, T, NCH, LANES), F32),
            pltpu.VMEM((HV, T, NCH, LANES), F32),
            pltpu.VMEM((HV, T, LANES), F32),
            pltpu.VMEM((HV, MODES, LANES), F32),
            pltpu.VMEM((HV, MODES * NCH, LANES), F32),
            pltpu.VMEM((HV, MODES * NCH, LANES), F32),
            pltpu.VMEM((HV, MODES * NCH, LANES), F32),
            pltpu.VMEM((HV, ROWS, LANES), F32),
            pltpu.VMEM((ROWS, CHL), BF16),
            pltpu.VMEM((ZH, Y, ROWS, CHL), BF16),
            pltpu.VMEM((CORES, X * ZL, N_TP, HALO, CHL), BF16),
            pltpu.VMEM((Y - 1, HALO, CHL), BF16),
            pltpu.VMEM((ROWS, FEAT), F32),
            pltpu.VMEM((2, MODES, CHL), F32),
            pltpu.VMEM((ZL, MODES, CHL), F32),
            pltpu.VMEM((X, MODES, CHL), F32),
            pltpu.VMEM((MODES, CHL), F32),
            dma((5, 2, 4)), dma((5, 2, 4)),
            dma((6, 2, 4)), dma((6, 2, 4)),
            dma((ZH, Y)), dma((ZH, Y)),
            dma((3 * Y - 2,)), dma((3 * Y - 2,)),
            dma((2, ZL - 1)), dma((2, ZL - 1)),
            dma((2, X - 1)), dma((2, X - 1)),
            dma((2,)), dma((2,)),
            dma((ZL + X - 1,)), dma((ZL + X - 1,)),
            dma((8,)),
        ],
        compiler_params=pltpu.CompilerParams(
            collective_id=0, has_side_effects=True, vmem_limit_bytes=56 * 1024 * 1024
        ),
        name="hyena",
    )(
        tokens,
        norm_gain.reshape(D // LANES, LANES),
        w_in.transpose(1, 0, 2),
        w_short,
        residues.T,
        decays.T,
        direct.reshape(1, CHL),
        w_out,
    )


def solution(mesh):
    placed = (
        P("ctx", "tp"),
        P(),
        P(None, None, "tp"),
        P(None, None, "tp"),
        P("tp", None),
        P("tp", None),
        P("tp"),
        P("tp", None),
    )
    return jax.shard_map(local, mesh=mesh, in_specs=placed, out_specs=P("ctx", "tp"), check_vma=False)
```

```python
import jax
import jax.numpy as jnp
from jax import lax
from jax.experimental import pallas as pl
from jax.experimental.pallas import tpu as pltpu
from jax.sharding import PartitionSpec as P

MESH = pl.DeviceIdType.MESH
F32 = jnp.float32
BF16 = jnp.bfloat16

X, ZL, CORES = 4, 4, 2
ZH, Y = 2, 4
N_CTX = X * ZL * CORES
N_TP = ZH * Y
ROWS = 512
FEAT = 512
D = 4096
CHL = 256
MODES = 16
GATED = 4
HALO = 16
EXT = ROWS + HALO
T = 16
NCH = ROWS // T
LANES = 128
HV = CHL // LANES


def remote(src, dst, send, recv, device):
    return pltpu.make_async_remote_copy(
        src_ref=src, dst_ref=dst, send_sem=send, recv_sem=recv, device_id=device, device_id_type=MESH
    )


def kernel(
    tok_in, gain_in, w_in, taps_in, res_in, dec_in, direct_in, w_out, out,
    gain, w_short, res, dec, direct,
    xg, halo, wv, xs, ssq, acc, pb, qb, xb, yb, ft, ab, eb, sb, pw, gb, own, gg, wo, wt, oacc,
    st_core, st_z, st_x, st_in,
    s1, r1, s2, r2, hs, hr, ws, wr, zs, zr, xsnd, xrcv, cs, cr, es, er, lsem,
):
    ctx = lax.axis_index("ctx")
    tp = lax.axis_index("tp")
    x, zl, core = ctx // (ZL * CORES), (ctx // CORES) % ZL, ctx % CORES
    zh, y = tp // Y, tp % Y

    def at_ctx(xx, zz, cc):
        return ((xx * ZL + zz) * CORES + cc, tp)

    def at_tp(hh, yy):
        return (ctx, hh * Y + yy)

    right, left = at_tp(zh, (y + 1) % Y), at_tp(zh, (y + Y - 1) % Y)
    across = at_tp(1 - zh, y)
    y_dev = [at_tp(zh, (y + b) % Y) for b in range(1, Y)]
    z_dev = [at_ctx(x, (zl + b) % ZL, core) for b in range(1, ZL)]
    x_dev = [at_ctx((x + a) % X, zl, core) for a in range(1, X)]
    other = at_ctx(x, zl, 1 - core)
    after = ((ctx + 1) % N_CTX, tp)
    before = ((ctx + N_CTX - 1) % N_CTX, tp)

    barrier = pltpu.get_barrier_semaphore()
    greeted = [across] + z_dev + x_dev + y_dev + [before, after, other]
    for device in greeted:
        pl.semaphore_signal(barrier, inc=1, device_id=device, device_id_type=MESH)
    small = [(gain_in, gain), (taps_in, w_short), (res_in, res), (dec_in, dec), (direct_in, direct)]
    tok = xg.at[0, 0]
    loads = [pltpu.make_async_copy(a, b, lsem.at[2 + i]) for i, (a, b) in enumerate([(tok_in, tok)] + small)]
    for load in loads:
        load.start()
    w_load = pltpu.make_async_copy(w_in, wv, lsem.at[0])
    w_load.start()
    for load in loads:
        load.wait()
    pl.semaphore_wait(barrier, len(greeted))

    class Gather:
        def __init__(self, mine, buf, send, recv, pieces, window, crossing, direct=False):
            self.mine, self.buf, self.send, self.recv = mine, buf, send, recv
            self.pieces, self.window, self.crossing = pieces, window, crossing
            self.queue = []
            self.direct = direct

        def straight(self, p, c):
            return self.direct and (p, c) == (1, self.pieces - 1)

        def rows(self, c, half=None):
            size = ROWS // self.pieces
            start = ROWS - size * (c + 1)
            return pl.ds(start, size) if half is None else pl.ds(start + half * (size // 2), size // 2)

        def held(self, p, s):
            return self.mine if (p, s) == (0, 0) else self.buf.at[p, s]

        def copy(self, kind, p, c):
            if kind == 0:
                src, dst, dev = self.held(p, 0).at[self.rows(c)], self.buf.at[p, 1, self.rows(c)], right
            elif kind == 1:
                src, dst, dev = self.held(p, 0).at[self.rows(c)], self.buf.at[p, 3, self.rows(c)], left
            elif kind == 2:
                src, dst, dev = self.buf.at[p, 1, self.rows(c, 0)], self.buf.at[p, 2, self.rows(c, 0)], right
            elif kind == 3:
                src, dst, dev = self.buf.at[p, 3, self.rows(c, 1)], self.buf.at[p, 2, self.rows(c, 1)], left
            elif kind == 5:
                src, dst, dev = self.held(p, 0).at[self.rows(c)], self.buf.at[p, 2, self.rows(c)], y_dev[1]
            else:
                src, dst, dev = self.mine.at[self.rows(c)], self.buf.at[1, 0, self.rows(c)], across
            return remote(src, dst, self.send.at[kind, p, c], self.recv.at[kind, p, c], dev)

        def push(self, *copies):
            if len(self.queue) >= self.window:
                for copy in self.queue[-self.window]:
                    copy.wait_send()
            for copy in copies:
                copy.start()
            self.queue.append(copies)

        def cross(self, c):
            if c >= self.crossing:
                self.copy(4, 0, c - self.crossing).wait_send()
            self.copy(4, 0, c).start()

        def spread(self, p, c):
            if p == 1:
                self.copy(4, 0, c).wait_recv()
            more = [self.copy(5, p, c)] if self.straight(p, c) else []
            self.push(self.copy(0, p, c), self.copy(1, p, c), *more)

        def forward(self, p, c):
            self.copy(0, p, c).wait_recv()
            self.copy(1, p, c).wait_recv()
            if not self.straight(p, c):
                self.push(self.copy(2, p, c), self.copy(3, p, c))

        def arrive(self, p, c):
            for kind in (5,) if self.straight(p, c) else (2, 3):
                self.copy(kind, p, c).wait_recv()

        def sent(self):
            for c in range(self.pieces - self.crossing, self.pieces):
                self.copy(4, 0, c).wait_send()
            for copies in self.queue[-self.window:]:
                for copy in copies:
                    copy.wait_send()

    def owner(p, s):
        return (zh + p) % ZH * Y + (y + (0, Y - 1, 2, 1)[s]) % Y

    tokens = Gather(tok, xg, s1, r1, 4, 2, 1)

    def halo_copy(p, s):
        return remote(
            tokens.held(p, s).at[pl.ds(ROWS - HALO, HALO)], halo.at[p, s], hs.at[p, s], hr.at[p, s], after
        )

    chip = x * ZL + zl

    wo_rows = pl.ds(pl.multiple_of(chip * HALO, HALO), HALO)

    def wo_columns(device):
        return w_out.at[wo_rows, pl.ds(pl.multiple_of(device[1] * FEAT + core * CHL, CHL), CHL)]

    def wo_across(b):
        dst = wt.at[b - 1] if b else wo.at[core, chip, tp]
        return remote(wo_columns(at_tp(1 - zh, (y + b) % Y)), dst, ws.at[b], wr.at[b], across)

    def wo_y(b):
        dst = wo.at[core, chip, tp]
        return remote(wo_columns(y_dev[b - 1]), dst, ws.at[Y + b - 1], wr.at[Y + b - 1], y_dev[b - 1])

    def wo_relayed(b):
        dst = wo.at[core, chip, across[1]]
        at = 2 * Y + b - 2
        return remote(wt.at[b - 1], dst, ws.at[at], wr.at[at], y_dev[b - 1])

    def wo_mine():
        return pltpu.make_async_copy(wo_columns((ctx, tp)), wo.at[core, chip, tp], lsem.at[1])

    def groups(part):
        return pl.ds(part * (N_TP // 2), N_TP // 2)

    def wo_z(part):
        block = wo.at[core, chip, groups(part)]
        return [remote(block, block, zs.at[part, i], zr.at[part, i], z_dev[i]) for i in range(ZL - 1)]

    def wo_x(part):
        block = wo.at[core, pl.ds(x * ZL, ZL), groups(part)]
        return [remote(block, block, xsnd.at[part, i], xrcv.at[part, i], x_dev[i]) for i in range(X - 1)]

    def start(copies):
        for copy in copies:
            copy.start()

    def landed(copies):
        for copy in copies:
            copy.wait_recv()

    def left_here(copies):
        for copy in copies:
            copy.wait_send()

    def wo_core(part):
        block = wo.at[core, :, groups(part)]
        return [remote(block, block, cs.at[part], cr.at[part], other)]

    def project(p, s, lo=0, hi=EXT):
        k = owner(p, s)
        block = tokens.held(p, s)
        scale = jnp.concatenate([gain[pl.ds(4 * k + i, 1), :] for i in range(4)], axis=1)
        if lo == 0:
            halo_copy(p, s).wait_recv()
            head = halo[p, s].astype(F32)
            xs[0:HALO, :] = (head * scale).astype(BF16)
            ssq[0:HALO, :] += sum(jnp.square(head[:, LANES * i:LANES * (i + 1)]) for i in range(4))

        @pl.loop(max(lo - HALO, 0) // 64, (hi - HALO) // 64)
        def _(i):
            at = pl.ds(pl.multiple_of(i * 64, 64), 64)
            to = pl.ds(pl.multiple_of(i * 64 + HALO, HALO), 64)
            values = block[at, :].astype(F32)
            xs[to, :] = (values * scale).astype(BF16)
            ssq[to, :] += sum(jnp.square(values[:, LANES * j:LANES * (j + 1)]) for j in range(4))

        @pl.loop(0, 3)
        def _(g):
            weights = wv[g, pl.ds(pl.multiple_of(k * FEAT, FEAT), FEAT), :]
            acc[g, lo:hi] += jnp.dot(xs[lo:hi], weights, preferred_element_type=F32)

    tokens.cross(0)
    tokens.spread(0, 0)
    tokens.spread(0, 1)
    halo_copy(0, 0).start()

    ssq[...] = jnp.zeros_like(ssq)
    acc[...] = jnp.zeros_like(acc)
    rate = dec[...]
    weight = res[...]
    powers = []
    for lag in range(T):
        row = jnp.sum(weight * jnp.exp(-rate * float(lag)), axis=0, keepdims=True)
        if lag == 0:
            row = row + direct[...]
        for h in range(HV):
            ft[h, lag:lag + 1, :] = row[:, LANES * h:LANES * (h + 1)]
    decay1 = jnp.exp(-rate)
    for h in range(HV):
        ab[h] = decay1[:, LANES * h:LANES * (h + 1)]

    @pl.loop(0, NCH)
    def _(n):
        table = res[...] * jnp.exp(-dec[...] * (T * n + 1).astype(F32))
        for h in range(HV):
            pw[h, pl.ds(pl.multiple_of(n * MODES, MODES), MODES), :] = table[:, LANES * h:LANES * (h + 1)]


    tokens.spread(0, 2)
    tokens.forward(0, 0)
    halo_copy(0, 1).start()
    halo_copy(0, 3).start()
    tokens.cross(1)
    w_load.wait()
    project(0, 0)
    tokens.spread(0, 3)
    tokens.forward(0, 1)
    tokens.arrive(0, 0)
    halo_copy(0, 2).start()
    tokens.cross(2)
    tokens.forward(0, 2)
    tokens.forward(0, 3)
    tokens.spread(1, 0)
    halo_copy(1, 0).start()
    project(0, 1)
    tokens.spread(1, 1)
    tokens.cross(3)
    project(0, 3)
    for c in range(1, 4):
        tokens.arrive(0, c)
    project(0, 2)
    tokens.forward(1, 0)
    halo_copy(1, 1).start()
    halo_copy(1, 3).start()
    tokens.spread(1, 2)
    tokens.forward(1, 1)
    tokens.arrive(1, 0)
    halo_copy(1, 2).start()
    for b in range(Y):
        wo_across(b).start()
    for b in range(1, Y):
        wo_y(b).start()
    wo_mine().start()
    tokens.spread(1, 3)
    project(1, 0)
    tokens.forward(1, 2)
    for b in range(1, Y):
        wo_across(b).wait_recv()
        wo_relayed(b).start()
    tokens.forward(1, 3)
    project(1, 1)
    project(1, 3)
    wo_mine().wait()
    wo_across(0).wait_recv()
    for b in range(1, Y):
        wo_y(b).wait_recv()
        wo_relayed(b).wait_recv()
    start(wo_z(0) + wo_z(1))
    tokens.arrive(1, 1)
    tokens.arrive(1, 2)
    project(1, 2, HALO + ROWS // 4, EXT)
    tokens.arrive(1, 3)
    project(1, 2, 0, HALO + ROWS // 4)

    inverse = lax.rsqrt(jnp.sum(ssq[...], axis=1, keepdims=True) * (1.0 / D) + 1e-06)
    row_id = lax.broadcasted_iota(jnp.int32, (EXT, 1), 0)
    inverse = jnp.where((row_id < HALO) & (ctx == 0), 0.0, inverse)
    for g in range(3):
        for h in range(HV):
            pb[g, h] = (acc[g, :, LANES * h:LANES * (h + 1)] * inverse).astype(BF16).astype(F32)

    for h in range(HV):
        lanes = pl.ds(LANES * h, LANES)
        taps = [[w_short[j, pl.ds(g, 1), lanes] for j in range(3)] for g in range(3)]

        def plane(g, t):
            return pb[g, h, pl.ds(HALO + t, NCH, stride=T), :]

        def filtered(t, kept):
            streams, keep = [], []
            for g in range(3):
                now = plane(g, t)
                older, old = kept[2 * g:2 * g + 2]
                streams.append(taps[g][0] * now + taps[g][1] * old + taps[g][2] * older)
                keep += [old, now]
            qb[h, t] = streams[0]
            xb[h, t] = streams[1] * streams[2]
            return tuple(keep)

        lax.fori_loop(0, T, filtered, tuple(plane(g, t) for g in range(3) for t in (-2, -1)), unroll=8)

    group = 4
    for h in range(HV):
        for r0 in range(0, MODES, group):
            factors = [jnp.broadcast_to(ab[h, r:r + 1, :], (NCH, LANES)) for r in range(r0, r0 + group)]

            def step(t, states):
                value = xb[h, t]
                return tuple(f * s + value for f, s in zip(factors, states))

            states = lax.fori_loop(0, T, step, tuple(jnp.zeros((NCH, LANES), F32) for _ in factors), unroll=8)
            for i, s in enumerate(states):
                eb[h, (r0 + i) * NCH:(r0 + i + 1) * NCH, :] = s

    block_end = []
    for h in range(HV):
        chunk_decay = jnp.exp(-dec[:, LANES * h:LANES * (h + 1)] * float(T))

        def scan(n, state):
            sb[h, pl.ds(pl.multiple_of(n * MODES, MODES), MODES), :] = state
            return chunk_decay * state + eb[h, pl.ds(n, MODES, stride=NCH), :]

        block_end.append(lax.fori_loop(0, NCH, scan, jnp.zeros((MODES, LANES), F32), unroll=8))
    mine = jnp.concatenate(block_end, axis=1)

    st_core[0] = mine
    core_copy = remote(st_core.at[0], st_core.at[1], es.at[0], er.at[0], other)
    core_copy.start()
    decay_block = jnp.exp(-dec[...] * float(ROWS))
    decay_chip = jnp.exp(-dec[...] * float(ROWS * CORES))
    decay_line = jnp.exp(-dec[...] * float(ROWS * CORES * ZL))
    core_copy.wait_recv()
    theirs = st_core[1]
    st_z[0] = jnp.where(core == 0, decay_block * mine + theirs, decay_block * theirs + mine)
    z_copies = [
        remote(st_z.at[0], st_z.at[b], es.at[b], er.at[b], z_dev[b - 1]) for b in range(1, ZL)
    ]
    for copy in z_copies:
        copy.start()

    def within(h):
        for t in range(T):
            total = None
            for lag in range(t + 1):
                term = ft[h, lag:lag + 1, :] * xb[h, t - lag]
                total = term if total is None else total + term
            yb[h, t] = total

    for h in range(HV):
        front = res[:, LANES * h:LANES * (h + 1)] * ab[h]

        @pl.loop(0, NCH)
        def _(n):
            at = pl.ds(pl.multiple_of(n * MODES, MODES), MODES)
            sb[h, at, :] = front * sb[h, at, :]

    within(0)
    for copy in z_copies:
        copy.wait_recv()
    line_end = jnp.zeros((MODES, CHL), F32)
    chip_in = jnp.zeros((MODES, CHL), F32)
    for zz in range(ZL):
        for b in range(ZL):
            here = (zl + ZL - b) % ZL == zz
            piece = st_z[b]
            if b == 0:
                chosen = jnp.where(here, piece, 0.0)
            else:
                chosen = jnp.where(here, piece, chosen)
        line_end = decay_chip * line_end + chosen
        chip_in = jnp.where(zz < zl, decay_chip * chip_in + chosen, chip_in)
    st_x[0] = line_end
    x_copies = [
        remote(st_x.at[0], st_x.at[a], es.at[ZL + a - 1], er.at[ZL + a - 1], x_dev[a - 1]) for a in range(1, X)
    ]
    for copy in x_copies:
        copy.start()
    within(1)
    before_chip = jnp.exp(-dec[...] * (ROWS * CORES * zl).astype(F32))
    for copy in x_copies:
        copy.wait_recv()
    line_in = jnp.zeros((MODES, CHL), F32)
    for xx in range(X):
        for a in range(X):
            here = (x + X - a) % X == xx
            piece = st_x[a]
            if a == 0:
                chosen = jnp.where(here, piece, 0.0)
            else:
                chosen = jnp.where(here, piece, chosen)
        line_in = jnp.where(xx < x, decay_line * line_in + chosen, line_in)
    chip_in = chip_in + before_chip * line_in
    carried = jnp.where(core == 0, chip_in, decay_block * chip_in + theirs)

    st_in[...] = carried
    per = NCH // GATED
    span = ROWS // GATED

    def gate(c):
        n0 = per * (GATED - 1 - c)
        for h in range(HV):
            lanes = pl.ds(LANES * h, LANES)
            factors, terms0 = [], []
            for r in range(MODES):
                at = pl.ds(n0 * MODES + r, per, stride=MODES)
                factors.append(jnp.broadcast_to(ab[h, r:r + 1, :], (per, LANES)))
                terms0.append(sb[h, at, :] + pw[h, at, :] * st_in[r:r + 1, lanes])

            def step(t, terms):
                sums = list(terms)
                while len(sums) > 1:
                    sums = [a + b for a, b in zip(sums[::2], sums[1::2])]
                total = yb[h, t, pl.ds(n0, per), :] + sums[0]
                gb[h, pl.ds(n0 * T + t, per, stride=T), :] = qb[h, t, pl.ds(n0, per), :] * total
                return tuple(f * s for f, s in zip(factors, terms))

            lax.fori_loop(0, T, step, tuple(terms0), unroll=8)
        for h in range(HV):
            at = pl.ds(ROWS - span * (c + 1), span)
            own[at, LANES * h:LANES * (h + 1)] = gb[h, at, :].astype(BF16)

    gates = Gather(own, gg, s2, r2, 4, 4, 1, direct=True)

    def emit(p, s, first=False, last=False):
        k = owner(p, s)
        block = gates.held(p, s)[...]
        for half in range(CORES):
            weights = wo[half, :, k].reshape(CHL, CHL)
            value = jnp.dot(block, weights, preferred_element_type=F32)
            lanes = slice(CHL * half, CHL * (half + 1))
            if first:
                oacc[:, lanes] = value
            elif last:
                out[:, lanes] = (oacc[:, lanes] + value).astype(BF16)
            else:
                oacc[:, lanes] += value

    gate(0)
    gates.cross(0)
    gates.spread(0, 0)
    landed(wo_z(0) + wo_z(1))
    start(wo_x(0) + wo_x(1))
    gate(1)
    gates.spread(0, 1)
    gate(2)
    gate(3)
    gates.spread(0, 2)
    gates.cross(1)
    gates.forward(0, 0)
    gates.spread(0, 3)
    gates.forward(0, 1)
    gates.cross(2)
    gates.forward(0, 2)
    gates.spread(1, 0)
    gates.forward(0, 3)
    gates.cross(3)
    gates.spread(1, 1)
    gates.forward(1, 0)
    landed(wo_x(0) + wo_x(1))
    start(wo_core(0) + wo_core(1))
    for c in range(4):
        gates.arrive(0, c)
    gates.spread(1, 2)
    landed(wo_core(0) + wo_core(1))
    emit(0, 0, first=True)
    gates.forward(1, 1)
    emit(0, 1)
    emit(0, 3)
    gates.spread(1, 3)
    emit(0, 2)
    emit(1, 0)
    gates.forward(1, 2)
    gates.forward(1, 3)
    emit(1, 1)
    emit(1, 3)
    for c in range(4):
        gates.arrive(1, c)
    emit(1, 2, last=True)

    tokens.sent()
    gates.sent()
    for p in range(ZH):
        for s in range(Y):
            halo_copy(p, s).wait_send()
    for b in range(Y):
        wo_across(b).wait_send()
    for b in range(1, Y):
        wo_y(b).wait_send()
        wo_relayed(b).wait_send()
    for part in range(2):
        left_here(wo_z(part) + wo_x(part) + wo_core(part))
    core_copy.wait_send()
    for copy in z_copies + x_copies:
        copy.wait_send()


def local(tokens, norm_gain, w_in, w_short, residues, decays, direct, w_out):
    dma = pltpu.SemaphoreType.DMA
    vmem = pl.BlockSpec(memory_space=pltpu.VMEM)
    hbm = pl.BlockSpec(memory_space=pl.ANY)
    return pl.pallas_call(
        kernel,
        out_shape=pltpu.VMEM((ROWS, FEAT), BF16),
        in_specs=[hbm] * 8,
        out_specs=vmem,
        scratch_shapes=[
            pltpu.VMEM((D // LANES, LANES), F32),
            pltpu.VMEM((3, 3, CHL), F32),
            pltpu.VMEM((MODES, CHL), F32),
            pltpu.VMEM((MODES, CHL), F32),
            pltpu.VMEM((1, CHL), F32),
            pltpu.VMEM((ZH, Y, ROWS, FEAT), BF16),
            pltpu.VMEM((ZH, Y, HALO, FEAT), BF16),
            pltpu.VMEM((3, D, CHL), BF16),
            pltpu.VMEM((EXT, FEAT), BF16),
            pltpu.VMEM((EXT, LANES), F32),
            pltpu.VMEM((3, EXT, CHL), F32),
            pltpu.VMEM((3, HV, EXT, LANES), F32),
            pltpu.VMEM((HV, T, NCH, LANES), F32),
            pltpu.VMEM((HV, T, NCH, LANES), F32),
            pltpu.VMEM((HV, T, NCH, LANES), F32),
            pltpu.VMEM((HV, T, LANES), F32),
            pltpu.VMEM((HV, MODES, LANES), F32),
            pltpu.VMEM((HV, MODES * NCH, LANES), F32),
            pltpu.VMEM((HV, MODES * NCH, LANES), F32),
            pltpu.VMEM((HV, MODES * NCH, LANES), F32),
            pltpu.VMEM((HV, ROWS, LANES), F32),
            pltpu.VMEM((ROWS, CHL), BF16),
            pltpu.VMEM((ZH, Y, ROWS, CHL), BF16),
            pltpu.VMEM((CORES, X * ZL, N_TP, HALO, CHL), BF16),
            pltpu.VMEM((Y - 1, HALO, CHL), BF16),
            pltpu.VMEM((ROWS, FEAT), F32),
            pltpu.VMEM((2, MODES, CHL), F32),
            pltpu.VMEM((ZL, MODES, CHL), F32),
            pltpu.VMEM((X, MODES, CHL), F32),
            pltpu.VMEM((MODES, CHL), F32),
            dma((5, 2, 4)), dma((5, 2, 4)),
            dma((6, 2, 4)), dma((6, 2, 4)),
            dma((ZH, Y)), dma((ZH, Y)),
            dma((3 * Y - 2,)), dma((3 * Y - 2,)),
            dma((2, ZL - 1)), dma((2, ZL - 1)),
            dma((2, X - 1)), dma((2, X - 1)),
            dma((2,)), dma((2,)),
            dma((ZL + X - 1,)), dma((ZL + X - 1,)),
            dma((8,)),
        ],
        compiler_params=pltpu.CompilerParams(
            collective_id=0, has_side_effects=True, vmem_limit_bytes=56 * 1024 * 1024
        ),
        name="hyena",
    )(
        tokens,
        norm_gain.reshape(D // LANES, LANES),
        w_in.transpose(1, 0, 2),
        w_short,
        residues.T,
        decays.T,
        direct.reshape(1, CHL),
        w_out,
    )


def solution(mesh):
    placed = (
        P("ctx", "tp"),
        P(),
        P(None, None, "tp"),
        P(None, None, "tp"),
        P("tp", None),
        P("tp", None),
        P("tp"),
        P("tp", None),
    )
    return jax.shard_map(local, mesh=mesh, in_specs=placed, out_specs=P("ctx", "tp"), check_vma=False)
```
